512 devices in a mesh: leaf: 512 (over x, z, y, core).
Axes of the slice: x: 4, y: 8, z: 8, core: 2. Of those that a mesh axis runs over, the one named last changes fastest.
Arguments:
- rhs: bfloat16 [524288, 128], P('leaf'), may hold values from -18 to 18
- diag_blocks: bfloat16 [1024, 512, 512], P('leaf'), may hold values from -4 to 4, as said below
- leaf_bases: bfloat16 [1024, 512, 256], P('leaf'), may hold values from -0.25 to 0.25
- leaf_up: bfloat16 [1024, 256, 256], P('leaf'), may hold values from -0.375 to 0.375
- chain_up: bfloat16 [512, 8, 256, 256], P('leaf'), may hold values from -6 to 6
- chain_pair: bfloat16 [512, 10, 256, 256], P('leaf'), may hold values from -6 to 6
- node_ranks: int32 [512, 11], P('leaf'), may hold values from 64 to 256, as said below
Outputs:
- solution: bfloat16 [524288, 128], P('leaf')
- residual: bfloat16 [524288, 128], P('leaf')
The draws below stay inside these ranges and needn't reach their ends.
Inputs may be any that keep to these rules, and one draw needn't show every extreme that they name: `node_ranks`: column 0 and 1 hold the ranks of leaves 2d and 2d + 1 of device d, column 2 + j the rank of the level j + 1 node above them; devices under one node hold the same rank for it, and the matrices of chain_up and chain_pair likewise agree for one node or pair. `diag_blocks`: each block is symmetric.
All inputs are finite; a program needn't handle non-finite values.
Results may differ from the reference program's by a relative error of at most 0.025.
Values may be sent and summed in bfloat16 or wider, within the bound.
A program may use at most 64 MiB of HBM per device.

```python
import math
import jax
import jax.numpy as jnp
from jax import lax

LEAF = 512
R = 256
NRHS = 128
ITERS = 4
LEVELS = 9
LEAVES = 1024
ORDER = 524288
N_LEAF = 512


def node_normals(key, slots, scale):
    device_ids = jnp.arange(N_LEAF, dtype=jnp.int32)
    node_ids = N_LEAF + device_ids[:, None] >> jnp.arange(slots, dtype=jnp.int32)[None, :]
    flat_ids = node_ids.reshape(-1)
    matrices = jax.vmap(lambda node: jnp.clip(jax.random.normal(jax.random.fold_in(key, node), (R, R), jnp.float32), -6.0, 6.0))(flat_ids)
    return matrices.reshape(N_LEAF, slots, R, R) * scale


def draw_rhs(key, part):
    key = jax.random.fold_in(key, 11)
    row_scale = 1.0 + 2.0 * jnp.arange(ORDER, dtype=jnp.float32) / ORDER
    sample = jnp.clip(jax.random.normal(key, (ORDER, NRHS), jnp.float32), -6.0, 6.0)
    return (sample * row_scale[:, None]).astype(jnp.bfloat16)


def draw_diag_blocks(key, part):
    key = jax.random.fold_in(key, 12)
    key_jitter, key_lead = jax.random.split(key)
    jitter = jnp.clip(jax.random.normal(key_jitter, (LEAVES, LEAF, LEAF), jnp.float32), -6.0, 6.0)
    diagonal_part = jax.random.uniform(key_lead, (LEAVES, LEAF), jnp.float32, 1.5, 3.0)
    identity = (jnp.arange(LEAF)[:, None] == jnp.arange(LEAF)[None, :]).astype(jnp.float32)
    symmetric = (jitter + jnp.swapaxes(jitter, 1, 2)) * (0.5 / math.sqrt(2.0 * LEAF))
    return (diagonal_part[:, :, None] * identity[None] + symmetric).astype(jnp.bfloat16)


def draw_chain_up(key, part):
    key = jax.random.fold_in(key, 13)
    return node_normals(key, LEVELS - 1, 1.1 / math.sqrt(R)).astype(jnp.bfloat16)


def draw_chain_pair(key, part):
    key = jax.random.fold_in(key, 14)
    return node_normals(key, LEVELS + 1, 0.8 / math.sqrt(R)).astype(jnp.bfloat16)


def draw_node_ranks(key, part):
    key = jax.random.fold_in(key, 15)
    rank_table = jax.random.randint(key, (4 * N_LEAF,), R // 4, R + 1, jnp.int32)
    rank_table = rank_table.at[2].set(R).at[3].set(R // 4)
    device_ids = jnp.arange(N_LEAF, dtype=jnp.int32)
    leaf_ids = 2 * N_LEAF + 2 * device_ids[:, None] + jnp.arange(2, dtype=jnp.int32)[None, :]
    chain_ids = N_LEAF + device_ids[:, None] >> jnp.arange(LEVELS, dtype=jnp.int32)[None, :]
    return rank_table[jnp.concatenate([leaf_ids, chain_ids], axis=1)]


def shard_levels(key, extent, cuts, smallest, top_value):
    gain = 1.0
    for position, shards_of in cuts:
        heights = jax.random.uniform(jax.random.fold_in(jax.random.fold_in(key, 6), position), (shards_of,), jnp.float32, smallest / len(cuts), top_value / len(cuts))
        gain = gain * jnp.repeat(jnp.exp(heights), extent[position] // shards_of).reshape((-1,) + (1,) * (len(extent) - 1 - position))
    return gain


def normal_values(own_key, shape, spread, most, cuts=(), held_as=jnp.bfloat16):
    array = spread * jax.random.normal(own_key, shape, jnp.float32)
    if cuts:
        array = array * shard_levels(own_key, shape, cuts, -0.22, 0.18)
    return jnp.clip(array, -most, most).astype(held_as)


def setup_inputs(seed: int = 0) -> dict:
    key_of = jax.random.split(jax.random.key(seed), 8)
    return {
        "rhs": draw_rhs(jax.random.fold_in(key_of[7], 71), 0),
        "diag_blocks": draw_diag_blocks(jax.random.fold_in(key_of[7], 71), 0),
        "leaf_bases": normal_values(key_of[2], (LEAVES, LEAF, R), LEAF ** -0.5, 0.25, ((0, 512),)),
        "leaf_up": normal_values(key_of[3], (LEAVES, R, R), R ** -0.5, 0.375, ((0, 512),)),
        "chain_up": draw_chain_up(jax.random.fold_in(key_of[7], 71), 0),
        "chain_pair": draw_chain_pair(jax.random.fold_in(key_of[7], 71), 0),
        "node_ranks": draw_node_ranks(jax.random.fold_in(key_of[7], 71), 0),
    }


def keep_rows(values, limit):
    row_ids = lax.broadcasted_iota(jnp.int32, values.shape, values.ndim - 2)
    return jnp.where(row_ids < limit, values, jnp.zeros_like(values))


def batched(left_side, right_side):
    return jnp.einsum("bij,bjn->bin", left_side.astype(jnp.float32), right_side.astype(jnp.float32))


def transposed(matrices):
    return jnp.swapaxes(matrices, 1, 2)


def hss_apply(operand, diag_blocks, leaf_bases, leaf_up, chain_up, chain_pair, node_ranks):
    blocks = operand.reshape(LEAVES, LEAF, NRHS)
    near_part = lax.map(lambda item: jnp.dot(item[0], item[1], preferred_element_type=jnp.float32), (diag_blocks, blocks))
    leaf_rank = node_ranks[:, 0:2].reshape(LEAVES)[:, None, None]
    g_leaf = keep_rows(lax.map(lambda item: jnp.dot(item[0].T, item[1], preferred_element_type=jnp.float32), (leaf_bases, blocks)), leaf_rank).astype(jnp.bfloat16)
    leaf_pair = chain_pair[:, 0]
    halves = g_leaf.reshape(N_LEAF, 2, R, NRHS)
    c_leaf = jnp.stack([batched(leaf_pair, halves[:, 1]), batched(transposed(leaf_pair), halves[:, 0])], axis=1).reshape(LEAVES, R, NRHS)
    lifted = batched(transposed(leaf_up), g_leaf).reshape(N_LEAF, 2, R, NRHS)
    upward = keep_rows(lifted[:, 0] + lifted[:, 1], node_ranks[:, 2][:, None, None]).astype(jnp.bfloat16)
    couplings = []
    for height in range(LEVELS):
        stride = 2 ** height
        members = N_LEAF // stride
        coupling = chain_pair[::2 * stride, height + 1]
        halves = upward.reshape(members // 2, 2, R, NRHS)
        coupled = jnp.stack([batched(coupling, halves[:, 1]), batched(transposed(coupling), halves[:, 0])], axis=1)
        couplings.append(coupled.reshape(members, R, NRHS))
        if height < LEVELS - 1:
            lifted = batched(transposed(chain_up[::stride, height]), upward).reshape(members // 2, 2, R, NRHS)
            upward = keep_rows(lifted[:, 0] + lifted[:, 1], node_ranks[::2 * stride, 3 + height][:, None, None]).astype(jnp.bfloat16)
    top_stride = 2 ** (LEVELS - 1)
    downward = keep_rows(couplings[LEVELS - 1], node_ranks[::top_stride, 1 + LEVELS][:, None, None]).astype(jnp.bfloat16)
    for height in range(LEVELS - 2, -1, -1):
        stride = 2 ** height
        parent = jnp.repeat(downward, 2, axis=0)
        total = couplings[height] + batched(chain_up[::stride, height], parent)
        downward = keep_rows(total, node_ranks[::stride, 2 + height][:, None, None]).astype(jnp.bfloat16)
    parent = jnp.repeat(downward, 2, axis=0)
    f_leaf = keep_rows(c_leaf + batched(leaf_up, parent), leaf_rank).astype(jnp.bfloat16)
    far_part = lax.map(lambda item: jnp.dot(item[0], item[1], preferred_element_type=jnp.float32), (leaf_bases, f_leaf))
    return (near_part + far_part).reshape(ORDER, NRHS)


def reference(rhs, diag_blocks, leaf_bases, leaf_up, chain_up, chain_pair, node_ranks):
    residual = rhs.astype(jnp.float32)
    solution = jnp.zeros_like(residual)
    for iteration in range(ITERS):
        applied = hss_apply(residual.astype(jnp.bfloat16), diag_blocks, leaf_bases, leaf_up, chain_up, chain_pair, node_ranks)
        numerator = jnp.sum(residual * applied, axis=0)
        denominator = jnp.sum(applied * applied, axis=0)
        step_size = numerator / (denominator + 1e-6)
        solution = solution + step_size * residual
        residual = residual - step_size * applied
    return solution.astype(jnp.bfloat16), residual.astype(jnp.bfloat16)
```

```python
import jax
import jax.numpy as jnp
from jax import lax
from jax.experimental import pallas as pl
from jax.experimental.pallas import tpu as pltpu
from jax.sharding import PartitionSpec as P

ITERS = 4
LEAF = 512
R = 256
HALF = 64
SCALE = 2.0**-32
MESH = pl.DeviceIdType.MESH
F32 = jnp.float32
BF16 = jnp.bfloat16
FAR = sorted(range(1, 32), key=lambda j: -(2 * min(j // 8, 2) + min(j % 8, 4)))


def meet(offset):
    return offset.bit_length() - 1


def flipped(index, offset):
    bit = 0
    out = index
    while offset >> bit:
        if offset >> bit & 1:
            out = out + (1 - 2 * ((index // 2**bit) % 2)) * 2**bit
        bit += 1
    return out


def dot(left, right):
    return jnp.dot(left, right, preferred_element_type=F32)


def dot_t(left, right):
    return lax.dot_general(left, right, (((1,), (1,)), ((), ())), preferred_element_type=F32)


def flip(matrix):
    return matrix.astype(F32).T.astype(BF16)


def pack(rows):
    count = rows.shape[0] // 8
    low = rows[:, :128].reshape(count, 8, 128)
    high = rows[:, 128:].reshape(count, 8, 128)
    return jnp.concatenate([low, high], axis=1).astype(BF16)


def unpack(tiles):
    count = tiles.shape[0]
    low = tiles[:, :8].reshape(8 * count, 128)
    high = tiles[:, 8:].reshape(8 * count, 128)
    return jnp.concatenate([low, high], axis=1)


def padded(rows):
    return jnp.concatenate([rows, jnp.zeros_like(rows)], axis=0).astype(BF16)


def kernel(
    rhs, diag, bases, lup, cup, cpair, ranks, out,
    rhs_v, diag_v, raw_b, raw_l, bas, lu, w1, p0, cu, cp, xhalf, xin,
    bas_t, lu_t, p0_t, p1_t, emat, emat_t, efive, efive_t, vin, rin, vout, rout,
    r_s, u_s, sol_s, op_s, near_s, ochip,
    s1, d1, s2, d2, s3, d3, sb, db, sa, da1, da2, sa2,
    load_sem, xs_sem, xr_sem, ss, rs,
):
    me = lax.axis_index("leaf")
    core = me % 2
    ypos = (me // 2) % 8
    group = me // 16
    mate = me + 1 - 2 * core

    def yflip(j):
        return me + (flipped(ypos, j) - ypos) * 2

    def gflip(j):
        return me + (flipped(group, j) - group) * 16

    own2 = pl.ds(2 * core, 2)
    loads = [
        pltpu.make_async_copy(rhs, rhs_v, load_sem.at[0]),
        pltpu.make_async_copy(bases, raw_b, load_sem.at[1]),
        pltpu.make_async_copy(lup, raw_l, load_sem.at[2]),
        pltpu.make_async_copy(cup.at[0], cu, load_sem.at[3]),
        pltpu.make_async_copy(cpair.at[0], cp, load_sem.at[4]),
        pltpu.make_async_copy(diag, diag_v.at[own2], load_sem.at[5]),
    ]
    for load in loads:
        load.start()

    barrier = pltpu.get_barrier_semaphore()
    peers = [mate] + [yflip(j) for j in range(1, 8)] + [gflip(j) for j in range(1, 32)]
    for peer in peers:
        pl.semaphore_signal(barrier, inc=1, device_id=(peer,), device_id_type=MESH)
    pl.semaphore_wait(barrier, len(peers))

    def remote(src, dst, send, recv, target):
        return pltpu.make_async_remote_copy(
            src_ref=src, dst_ref=dst, send_sem=send, recv_sem=recv, device_id=(target,), device_id_type=MESH
        )

    lanes_w = lax.broadcasted_iota(jnp.int32, (R, R), 1)
    lanes_b = lax.broadcasted_iota(jnp.int32, (LEAF, R), 1)

    def masked(value, lanes, rank):
        return jnp.where(lanes < rank, value.astype(F32), 0.0).astype(BF16)

    loads[0].wait()
    turned = rhs_v[...].astype(F32).T.astype(BF16)
    for half in range(2):
        for leaf in range(2):
            xhalf[half, leaf] = turned[half * HALF:(half + 1) * HALF, leaf * LEAF:(leaf + 1) * LEAF]
    swaps = [remote(xhalf.at[1 - core], xin.at[own2], xs_sem.at[0], xr_sem.at[0], mate)]
    swaps[0].start()
    xin[own2] = xhalf[core]
    loads[1].wait()
    for leaf in range(2):
        bas[2 * core + leaf] = masked(raw_b[leaf], lanes_b, ranks[0, leaf])
    swaps.append(remote(bas.at[own2], bas.at[own2], xs_sem.at[1], xr_sem.at[1], mate))
    swaps[1].start()
    loads[2].wait()
    for leaf in range(2):
        lu[2 * core + leaf] = masked(raw_l[leaf], lanes_w, ranks[0, 2])
    swaps.append(remote(lu.at[own2], lu.at[own2], xs_sem.at[2], xr_sem.at[2], mate))
    swaps[2].start()
    loads[3].wait()
    own1 = pl.ds(core, 1)
    w1[core] = masked(cu[0], lanes_w, ranks[0, 3])
    swaps.append(remote(w1.at[own1], w1.at[own1], xs_sem.at[3], xr_sem.at[3], mate))
    swaps[3].start()
    loads[4].wait()
    p0[core] = cp[0]
    swaps.append(remote(p0.at[own1], p0.at[own1], xs_sem.at[4], xr_sem.at[4], mate))
    swaps[4].start()
    loads[5].wait()
    swaps.append(remote(diag_v.at[own2], diag_v.at[own2], xs_sem.at[5], xr_sem.at[5], mate))
    swaps[5].start()

    def transfer(level):
        return masked(cu[level - 1], lanes_w, ranks[0, level + 2])

    v3 = transfer(2)
    v4 = dot(v3, transfer(3)).astype(BF16)
    v5 = dot(v4, transfer(4)).astype(BF16)
    vin[:, 0:R] = v3
    vin[:, R:2 * R] = v4
    t = transfer(5)
    vout[:, 0:R] = t
    for level in range(6, 9):
        t = dot(t, transfer(level)).astype(BF16)
        vout[:, (level - 5) * R:(level - 4) * R] = t

    def oriented(level):
        left = (me // 2 ** (level - 1)) % 2 == 0
        return jnp.where(left, cp[level].astype(F32).T, cp[level].astype(F32)).astype(BF16)

    rin[0:R, :] = oriented(2)
    rin[R:2 * R, :] = dot_t(oriented(3), vin[:, 0:R]).astype(BF16)
    rin[2 * R:3 * R, :] = dot_t(oriented(4), vin[:, R:2 * R]).astype(BF16)
    rout[0:R, :] = oriented(5)
    for level in range(6, 10):
        at = (level - 6) * R
        rout[at + R:at + 2 * R, :] = dot_t(oriented(level), vout[:, at:at + R]).astype(BF16)
    p1_t[...] = flip(cp[1])

    for swap in swaps:
        swap.wait_recv()
    for dev in range(2):
        p0_t[dev] = flip(p0[dev])
    for leaf in range(4):
        base = bas[leaf]
        lift = lu[leaf]
        low = dot(lift, w1[leaf // 2]).astype(BF16)
        e2 = dot(base, low).astype(BF16)
        emat[leaf] = e2
        emat_t[leaf] = flip(e2)
        e5 = dot(base, dot(low, v5).astype(BF16)).astype(BF16)
        efive[leaf] = e5
        efive_t[leaf] = flip(e5)
        bas_t[leaf] = flip(base)
        lu_t[leaf] = flip(lift)
    first = xin[...].astype(F32)
    r_s[...] = first
    u_s[...] = first
    sol_s[...] = jnp.zeros_like(sol_s)
    op_s[...] = (first * SCALE).astype(BF16)

    lanes_a = lax.broadcasted_iota(jnp.int32, (8, 128), 1)

    def sums_start(k):
        r = r_s[...]
        u = u_s[...]
        num = jnp.sum(jnp.sum(r * u, axis=0), axis=1, keepdims=True)
        den = jnp.sum(jnp.sum(u * u, axis=0), axis=1, keepdims=True)
        tile = jnp.zeros((8, 128), F32)
        for a in range(8):
            tile = jnp.where(lanes_a == a, num[8 * a:8 * a + 8], tile)
            tile = jnp.where(lanes_a == 8 + a, den[8 * a:8 * a + 8], tile)
        sa[k] = tile
        for j in (4, 5, 3, 6, 2, 7, 1):
            remote(sa.at[k], da1.at[k, j], ss.at[4, k], rs.at[4, k], yflip(j)).start()

    def sums_middle(k):
        remote(da1.at[k, pl.ds(1, 7)], da1.at[k, pl.ds(1, 7)], ss.at[4, k], rs.at[4, k], mate).wait_recv()
        sa2[k] = sa[k] + jnp.sum(da1[k, 1:8], axis=0)
        for j in FAR:
            remote(sa2.at[k], da2.at[k, j], ss.at[5, k], rs.at[5, k], gflip(j)).start()

    def sums_end(k):
        remote(da2.at[k, pl.ds(1, 31)], da2.at[k, pl.ds(1, 31)], ss.at[5, k], rs.at[5, k], mate).wait_recv()
        tile = sa2[k] + jnp.sum(da2[k, 1:32], axis=0)
        steps = [tile[:, a:a + 1] / (tile[:, 8 + a:9 + a] + 1e-6) for a in range(8)]
        return jnp.concatenate(steps, axis=0)

    def sums_sent(k):
        remote(da1.at[k, pl.ds(1, 7)], da1.at[k, pl.ds(1, 7)], ss.at[4, k], rs.at[4, k], mate).wait_send()
        remote(da2.at[k, pl.ds(1, 31)], da2.at[k, pl.ds(1, 31)], ss.at[5, k], rs.at[5, k], mate).wait_send()

    def tree(k, carry):
        g5 = dot(op_s[0], efive[0])
        for leaf in range(1, 4):
            g5 = g5 + dot(op_s[leaf], efive[leaf])
        s1[k] = pack(g5)
        for j in (4, 5, 3, 6, 2, 7, 1):
            remote(s1.at[k, flipped(ypos, j)], d1.at[k, j], ss.at[0, k], rs.at[0, k], yflip(j)).start()
        sums_start(k)
        g2 = dot(op_s[0], emat[0])
        for leaf in range(1, 4):
            g2 = g2 + dot(op_s[leaf], emat[leaf])
        g2 = g2.astype(BF16)
        sb[k, 0] = g2
        lifted = dot(g2, vin[...]).astype(BF16)
        sb[k, 1] = lifted[:, :R]
        sb[k, 2] = lifted[:, R:]
        for j in range(1, 8):
            remote(sb.at[k, meet(j)], db.at[k, j], ss.at[3, k], rs.at[3, k], yflip(j)).start()
        for leaf in range(4):
            near_s[leaf] = dot(op_s[leaf], diag_v[leaf])
        remote(d1.at[k, pl.ds(1, 7)], d1.at[k, pl.ds(1, 7)], ss.at[0, k], rs.at[0, k], mate).wait_recv()
        mine = s1[k, ypos].astype(F32) + jnp.sum(d1[k, 1:8].astype(F32), axis=0)
        node = unpack(mine[None])
        s2[k, 0] = pack(node)[0]
        lifted = dot(padded(node), vout[...])[:8]
        for level in range(4):
            s2[k, level + 1] = pack(lifted[:, level * R:(level + 1) * R])[0]
        for j in FAR:
            remote(s2.at[k, meet(j)], d2.at[k, j], ss.at[1, k], rs.at[1, k], gflip(j)).start()
        sums_middle(k)
        g_leaf = [dot(op_s[leaf], bas[leaf]).astype(BF16) for leaf in range(4)]
        g_one = [
            (dot(g_leaf[2 * dev], lu[2 * dev]) + dot(g_leaf[2 * dev + 1], lu[2 * dev + 1])).astype(BF16)
            for dev in range(2)
        ]
        c_one = [dot(g_one[1], p1_t[...]).astype(BF16), dot(g_one[0], cp[1]).astype(BF16)]
        for dev in range(2):
            a, b = 2 * dev, 2 * dev + 1
            f_a = dot(g_leaf[b], p0_t[dev]) + dot(c_one[dev], lu_t[a])
            f_b = dot(g_leaf[a], p0[dev]) + dot(c_one[dev], lu_t[b])
            near_s[a] += dot(f_a.astype(BF16), bas_t[a])
            near_s[b] += dot(f_b.astype(BF16), bas_t[b])
        remote(db.at[k, pl.ds(1, 7)], db.at[k, pl.ds(1, 7)], ss.at[3, k], rs.at[3, k], mate).wait_recv()
        inner = dot(db[k, 1], rin[0:R, :])
        pair = db[k, 2].astype(F32) + db[k, 3].astype(F32)
        inner = inner + dot(pair.astype(BF16), rin[R:2 * R, :])
        quad = jnp.sum(db[k, 4:8].astype(F32), axis=0)
        inner = (inner + dot(quad.astype(BF16), rin[2 * R:3 * R, :])).astype(BF16)
        for leaf in range(4):
            near_s[leaf] += dot(inner, emat_t[leaf])
        remote(d2.at[k, pl.ds(1, 31)], d2.at[k, pl.ds(1, 31)], ss.at[1, k], rs.at[1, k], mate).wait_recv()
        got = [unpack(d2[k, 1].astype(F32)[None])]
        for level in range(1, 5):
            got.append(unpack(jnp.sum(d2[k, 2**level:2 ** (level + 1)].astype(F32), axis=0)[None]))
        f5 = dot(padded(jnp.concatenate(got, axis=1)), rout[...])[:8]
        s3[k] = pack(f5)[0]
        for j in (4, 5, 3, 6, 2, 7, 1):
            remote(s3.at[k], d3.at[k, ypos], ss.at[2, k], rs.at[2, k], yflip(j)).start()
        d3[k, ypos] = s3[k]
        step = sums_end(k)
        started = jnp.where(k == 0, 0.0, 1.0).astype(F32)
        gain = step * started
        back = (gain - (1.0 - started)) * (1.0 / SCALE)
        for leaf in range(4):
            u = u_s[leaf]
            r = r_s[leaf]
            sol_s[leaf] += gain * r
            r_s[leaf] = r - gain * u
            u_s[leaf] = started * u - back * near_s[leaf]
        remote(d3.at[k, pl.ds(1, 7)], d3.at[k, pl.ds(1, 7)], ss.at[2, k], rs.at[2, k], mate).wait_recv()
        far = unpack(d3[k].astype(F32)).astype(BF16)
        for leaf in range(4):
            u = u_s[leaf] - back * dot(far, efive_t[leaf])
            u_s[leaf] = u
            op_s[leaf] = (u * SCALE).astype(BF16)
        remote(s1.at[k, pl.ds(1, 7)], s1.at[k, pl.ds(1, 7)], ss.at[0, k], rs.at[0, k], mate).wait_send()
        remote(d2.at[k, pl.ds(1, 31)], d2.at[k, pl.ds(1, 31)], ss.at[1, k], rs.at[1, k], mate).wait_send()
        remote(d3.at[k, pl.ds(1, 7)], d3.at[k, pl.ds(1, 7)], ss.at[2, k], rs.at[2, k], mate).wait_send()
        remote(db.at[k, pl.ds(1, 7)], db.at[k, pl.ds(1, 7)], ss.at[3, k], rs.at[3, k], mate).wait_send()
        sums_sent(k)
        return carry

    lax.fori_loop(0, ITERS, tree, 0)

    sums_start(ITERS)
    sums_middle(ITERS)
    step = sums_end(ITERS)
    sums_sent(ITERS)
    for leaf in range(4):
        r = r_s[leaf]
        ochip[leaf, 0] = (sol_s[leaf] + step * r).astype(BF16)
        ochip[leaf, 1] = (r - step * u_s[leaf]).astype(BF16)
    theirs = pl.ds(2 * (1 - core), 2)
    swap = remote(ochip.at[theirs], out.at[core], xs_sem.at[6], xr_sem.at[6], mate)
    swap.start()
    here = pltpu.make_async_copy(ochip.at[own2], out.at[core], load_sem.at[6])
    here.start()
    here.wait()
    swap.wait_recv()
    swap.wait_send()
    for swap in swaps:
        swap.wait_send()


def per_device(rhs, diag_blocks, leaf_bases, leaf_up, chain_up, chain_pair, node_ranks):
    anywhere = pl.BlockSpec(memory_space=pl.ANY)
    vm = pltpu.VMEM
    dma = pltpu.SemaphoreType.DMA
    n = ITERS
    result = pl.pallas_call(
        kernel,
        out_shape=jax.ShapeDtypeStruct((2, 2, 2, HALF, LEAF), BF16),
        in_specs=[anywhere] * 6 + [pl.BlockSpec(memory_space=pltpu.SMEM)],
        out_specs=anywhere,
        scratch_shapes=[
            vm((2 * LEAF, 2 * HALF), BF16),
            vm((4, LEAF, LEAF), BF16),
            vm((2, LEAF, R), BF16),
            vm((2, R, R), BF16),
            vm((4, LEAF, R), BF16),
            vm((4, R, R), BF16),
            vm((2, R, R), BF16),
            vm((2, R, R), BF16),
            vm((8, R, R), BF16),
            vm((10, R, R), BF16),
            vm((2, 2, HALF, LEAF), BF16),
            vm((4, HALF, LEAF), BF16),
            vm((4, R, LEAF), BF16),
            vm((4, R, R), BF16),
            vm((2, R, R), BF16),
            vm((R, R), BF16),
            vm((4, LEAF, R), BF16),
            vm((4, R, LEAF), BF16),
            vm((4, LEAF, R), BF16),
            vm((4, R, LEAF), BF16),
            vm((R, 2 * R), BF16),
            vm((3 * R, R), BF16),
            vm((R, 4 * R), BF16),
            vm((5 * R, R), BF16),
            vm((4, HALF, LEAF), F32),
            vm((4, HALF, LEAF), F32),
            vm((4, HALF, LEAF), F32),
            vm((4, HALF, LEAF), BF16),
            vm((4, HALF, LEAF), F32),
            vm((4, 2, HALF, LEAF), BF16),
            vm((n, 8, 16, 128), BF16),
            vm((n, 8, 16, 128), BF16),
            vm((n, 5, 16, 128), BF16),
            vm((n, 32, 16, 128), BF16),
            vm((n, 16, 128), BF16),
            vm((n, 8, 16, 128), BF16),
            vm((n, 3, HALF, R), BF16),
            vm((n, 8, HALF, R), BF16),
            vm((n + 1, 8, 128), F32),
            vm((n + 1, 8, 8, 128), F32),
            vm((n + 1, 32, 8, 128), F32),
            vm((n + 1, 8, 128), F32),
            dma((7,)),
            dma((7,)),
            dma((7,)),
            dma((6, n + 1)),
            dma((6, n + 1)),
        ],
        compiler_params=pltpu.CompilerParams(
            collective_id=0, has_side_effects=True, vmem_limit_bytes=56 * 2**20
        ),
        name="sweeps",
    )(rhs, diag_blocks, leaf_bases, leaf_up, chain_up, chain_pair, node_ranks)
    result = result.transpose(2, 1, 4, 0, 3).reshape(2, 2 * LEAF, 2 * HALF)
    return result[0], result[1]


def solution(mesh):
    return jax.shard_map(
        per_device,
        mesh=mesh,
        in_specs=(
            P("leaf", None),
            P("leaf", None, None),
            P("leaf", None, None),
            P("leaf", None, None),
            P("leaf", None, None, None),
            P("leaf", None, None, None),
            P("leaf", None),
        ),
        out_specs=(P("leaf", None), P("leaf", None)),
        check_vma=False,
    )
```

```python
import jax
import jax.numpy as jnp
from jax import lax
from jax.experimental import pallas as pl
from jax.experimental.pallas import tpu as pltpu
from jax.sharding import PartitionSpec as P

ITERS = 4
LEAF = 512
R = 256
HALF = 64
SCALE = 2.0**-60
MESH = pl.DeviceIdType.MESH
F32 = jnp.float32
BF16 = jnp.bfloat16
FAR = sorted(range(1, 32), key=lambda j: -(2 * min(j // 8, 2) + min(j % 8, 4)))


PAIRS = [(i, j) for j in range(1, ITERS + 1) for i in range(j + 1)]
EARLY = [(m, i, j) for m, (i, j) in enumerate(PAIRS) if j < ITERS]
LATE = [(m, i, j) for m, (i, j) in enumerate(PAIRS) if j == ITERS]


def meet(offset):
    return offset.bit_length() - 1


def flipped(index, offset):
    bit = 0
    out = index
    while offset >> bit:
        if offset >> bit & 1:
            out = out + (1 - 2 * ((index // 2**bit) % 2)) * 2**bit
        bit += 1
    return out


def dot(left, right):
    return jnp.dot(left, right, preferred_element_type=F32)


def dot_t(left, right):
    return lax.dot_general(left, right, (((1,), (1,)), ((), ())), preferred_element_type=F32)


def flip(matrix):
    return matrix.astype(F32).T.astype(BF16)


def pack(rows):
    count = rows.shape[0] // 8
    low = rows[:, :128].reshape(count, 8, 128)
    high = rows[:, 128:].reshape(count, 8, 128)
    return jnp.concatenate([low, high], axis=1).astype(BF16)


def unpack(tiles):
    count = tiles.shape[0]
    low = tiles[:, :8].reshape(8 * count, 128)
    high = tiles[:, 8:].reshape(8 * count, 128)
    return jnp.concatenate([low, high], axis=1)


def padded(rows):
    return jnp.concatenate([rows, jnp.zeros_like(rows)], axis=0).astype(BF16)


def kernel(
    rhs, diag, bases, lup, cup, cpair, ranks, out_a, out_b,
    rhs_v, diag_v, raw_b, raw_l, bas, lu, w1, lowered, p0, cu, cp, xhalf, xin,
    bas_t, lu_t, p0_t, p1_t, emat, emat_t, efive, efive_t, vin, rin, vout, rout,
    ks, op_s, near_s, sig, sig_here, gt,
    s1, d1, s2, d2, s3, d3, sb, db, sa, da1, da2, sa2, hs, hd1, hd2, gs, omine, otheirs, outs_v,
    load_sem, xs_sem, xr_sem, ss, rs,
):
    me = lax.axis_index("leaf")
    core = me % 2
    ypos = (me // 2) % 8
    group = me // 16
    mate = me + 1 - 2 * core

    def yflip(j):
        return me + (flipped(ypos, j) - ypos) * 2

    def gflip(j):
        return me + (flipped(group, j) - group) * 16

    own2 = pl.ds(2 * core, 2)
    loads = [
        pltpu.make_async_copy(rhs, rhs_v, load_sem.at[0]),
        pltpu.make_async_copy(bases, raw_b, load_sem.at[1]),
        pltpu.make_async_copy(lup, raw_l, load_sem.at[2]),
        pltpu.make_async_copy(cup.at[0], cu, load_sem.at[3]),
        pltpu.make_async_copy(cpair.at[0], cp, load_sem.at[4]),
        pltpu.make_async_copy(diag, diag_v.at[own2], load_sem.at[5]),
    ]
    for load in loads:
        load.start()

    barrier = pltpu.get_barrier_semaphore()
    peers = [mate] + [yflip(j) for j in range(1, 8)] + [gflip(j) for j in range(1, 32)]
    for peer in peers:
        pl.semaphore_signal(barrier, inc=1, device_id=(peer,), device_id_type=MESH)
    pl.semaphore_wait(barrier, len(peers))

    def remote(src, dst, send, recv, target):
        return pltpu.make_async_remote_copy(
            src_ref=src, dst_ref=dst, send_sem=send, recv_sem=recv, device_id=(target,), device_id_type=MESH
        )

    lanes_w = lax.broadcasted_iota(jnp.int32, (R, R), 1)
    lanes_b = lax.broadcasted_iota(jnp.int32, (LEAF, R), 1)

    def masked(value, lanes, rank):
        return jnp.where(lanes < rank, value.astype(F32), 0.0).astype(BF16)

    loads[0].wait()
    turned = rhs_v[...].astype(F32).T.astype(BF16)
    for half in range(2):
        for leaf in range(2):
            xhalf[half, leaf] = turned[half * HALF:(half + 1) * HALF, leaf * LEAF:(leaf + 1) * LEAF]
    swaps = [remote(xhalf.at[1 - core], xin.at[own2], xs_sem.at[0], xr_sem.at[0], mate)]
    swaps[0].start()
    xin[own2] = xhalf[core]
    loads[1].wait()
    for leaf in range(2):
        bas[2 * core + leaf] = masked(raw_b[leaf], lanes_b, ranks[0, leaf])
    swaps.append(remote(bas.at[own2], bas.at[own2], xs_sem.at[1], xr_sem.at[1], mate))
    swaps[1].start()
    loads[2].wait()
    for leaf in range(2):
        lu[2 * core + leaf] = masked(raw_l[leaf], lanes_w, ranks[0, 2])
    swaps.append(remote(lu.at[own2], lu.at[own2], xs_sem.at[2], xr_sem.at[2], mate))
    swaps[2].start()
    loads[3].wait()
    own1 = pl.ds(core, 1)
    w1[core] = masked(cu[0], lanes_w, ranks[0, 3])
    swaps.append(remote(w1.at[own1], w1.at[own1], xs_sem.at[3], xr_sem.at[3], mate))
    swaps[3].start()
    loads[4].wait()
    p0[core] = cp[0]
    swaps.append(remote(p0.at[own1], p0.at[own1], xs_sem.at[4], xr_sem.at[4], mate))
    swaps[4].start()
    loads[5].wait()
    swaps.append(remote(diag_v.at[own2], diag_v.at[own2], xs_sem.at[5], xr_sem.at[5], mate))
    swaps[5].start()

    def transfer(level):
        return masked(cu[level - 1], lanes_w, ranks[0, level + 2])

    def oriented(level):
        left = (me // 2 ** (level - 1)) % 2 == 0
        return jnp.where(left, cp[level].astype(F32).T, cp[level].astype(F32)).astype(BF16)

    v3 = transfer(2)
    v4 = dot(v3, transfer(3)).astype(BF16)
    v5 = dot(v4, transfer(4)).astype(BF16)
    vin[:, 0:R] = v3
    vin[:, R:2 * R] = v4
    swaps[0].wait_recv()
    first = xin[...].astype(F32)
    ks[0] = first
    sig[...] = jnp.ones_like(sig)
    sig_here[...] = jnp.ones_like(sig_here)
    op_s[...] = (first * SCALE).astype(BF16)
    for swap in swaps[1:4]:
        swap.wait_recv()
    for leaf in range(4):
        low = dot(lu[leaf], w1[leaf // 2]).astype(BF16)
        lowered[leaf] = low
        efive[leaf] = dot(bas[leaf], dot(low, v5).astype(BF16)).astype(BF16)

    def to_group(k):
        for j in (4, 5, 3, 6, 2, 7, 1):
            remote(s1.at[k, flipped(ypos, j)], d1.at[k, j], ss.at[0, k], rs.at[0, k], yflip(j)).start()

    def from_group(k):
        remote(d1.at[k, pl.ds(1, 7)], d1.at[k, pl.ds(1, 7)], ss.at[0, k], rs.at[0, k], mate).wait_recv()
        return unpack((s1[k, ypos].astype(F32) + jnp.sum(d1[k, 1:8].astype(F32), axis=0))[None])

    def to_far(k, node):
        s2[k, 0] = pack(node)[0]
        lifted = dot(padded(node), vout[...])[:8]
        for level in range(4):
            s2[k, level + 1] = pack(lifted[:, level * R:(level + 1) * R])[0]
        for j in FAR:
            remote(s2.at[k, meet(j)], d2.at[k, j], ss.at[1, k], rs.at[1, k], gflip(j)).start()

    g5 = dot(op_s[0], efive[0])
    for leaf in range(1, 4):
        g5 = g5 + dot(op_s[leaf], efive[leaf])
    s1[0] = pack(g5)
    to_group(0)

    for leaf in range(4):
        emat[leaf] = dot(bas[leaf], lowered[leaf]).astype(BF16)

    def compose_rest():
        t = transfer(5)
        vout[:, 0:R] = t
        for level in range(6, 9):
            t = dot(t, transfer(level)).astype(BF16)
            vout[:, (level - 5) * R:(level - 4) * R] = t
        for leaf in range(4):
            efive_t[leaf] = flip(efive[leaf])
        gram = dot(efive_t[0], efive[0])
        for leaf in range(1, 4):
            gram = gram + dot(efive_t[leaf], efive[leaf])
        hs[...] = gram.astype(BF16).reshape(2, 8, 16, R)
        for j in (4, 5, 3, 6, 2, 7, 1):
            remote(hs.at[core, flipped(ypos, j)], hd1.at[j], xs_sem.at[7], xr_sem.at[7], yflip(j)).start()
        p1_t[...] = flip(cp[1])
        for swap in swaps[4:]:
            swap.wait_recv()
        for dev in range(2):
            p0_t[dev] = flip(p0[dev])
        for leaf in range(4):
            bas_t[leaf] = flip(bas[leaf])
            lu_t[leaf] = flip(lu[leaf])

    def compose_last():
        rin[0:R, :] = oriented(2)
        rin[R:2 * R, :] = dot_t(oriented(3), vin[:, 0:R]).astype(BF16)
        rin[2 * R:3 * R, :] = dot_t(oriented(4), vin[:, R:2 * R]).astype(BF16)
        for leaf in range(4):
            emat_t[leaf] = flip(emat[leaf])
        rout[0:R, :] = oriented(5)
        for level in range(6, 10):
            at = (level - 6) * R
            rout[at + R:at + 2 * R, :] = dot_t(oriented(level), vout[:, at:at + R]).astype(BF16)

    lane = lax.broadcasted_iota(jnp.int32, (8, 128), 1)

    def inner_products(pairs, tile):
        for m, left, right in pairs:
            got = ks[left, 0] * ks[right, 0]
            for leaf in range(1, 4):
                got = got + ks[left, leaf] * ks[right, leaf]
            got = jnp.sum(got, axis=1, keepdims=True)
            for a in range(8):
                tile = jnp.where(lane == 8 * m + a, got[8 * a:8 * a + 8], tile)
        return tile

    def sums_start(q, tile):
        sa[q] = tile
        for j in (4, 5, 3, 6, 2, 7, 1):
            remote(sa.at[q], da1.at[q, j], ss.at[4, q], rs.at[4, q], yflip(j)).start()

    def sums_middle(q):
        remote(da1.at[q, pl.ds(1, 7)], da1.at[q, pl.ds(1, 7)], ss.at[4, q], rs.at[4, q], mate).wait_recv()
        sa2[q] = sa[q] + jnp.sum(da1[q, 1:8], axis=0)
        for j in FAR:
            remote(sa2.at[q], da2.at[q, j], ss.at[5, q], rs.at[5, q], gflip(j)).start()

    def sums_end(q):
        remote(da2.at[q, pl.ds(1, 31)], da2.at[q, pl.ds(1, 31)], ss.at[5, q], rs.at[5, q], mate).wait_recv()
        return sa2[q] + jnp.sum(da2[q, 1:32], axis=0)

    def sums_sent(q):
        remote(da1.at[q, pl.ds(1, 7)], da1.at[q, pl.ds(1, 7)], ss.at[4, q], rs.at[4, q], mate).wait_send()
        remote(da2.at[q, pl.ds(1, 31)], da2.at[q, pl.ds(1, 31)], ss.at[5, q], rs.at[5, q], mate).wait_send()

    def place(tile, m):
        return tile if m == 0 else pltpu.roll(tile, 128 - 8 * m, 1)

    def by_column(tile):
        return jnp.concatenate([tile[:, a:a + 1] for a in range(8)], axis=0)

    def chip_part(x):
        g_leaf = [dot(x[leaf], bas[leaf]).astype(BF16) for leaf in range(4)]
        g_one = [
            (dot(g_leaf[2 * dev], lu[2 * dev]) + dot(g_leaf[2 * dev + 1], lu[2 * dev + 1])).astype(BF16)
            for dev in range(2)
        ]
        c_one = [dot(g_one[1], p1_t[...]).astype(BF16), dot(g_one[0], cp[1]).astype(BF16)]
        out = []
        for dev in range(2):
            a, b = 2 * dev, 2 * dev + 1
            f_a = dot(g_leaf[b], p0_t[dev]) + dot(c_one[dev], lu_t[a])
            f_b = dot(g_leaf[a], p0[dev]) + dot(c_one[dev], lu_t[b])
            out.append(dot(x[a], diag_v[a]) + dot(f_a.astype(BF16), bas_t[a]))
            out.append(dot(x[b], diag_v[b]) + dot(f_b.astype(BF16), bas_t[b]))
        return out

    def to_siblings(coefs, src, dst, send, recv):
        src[0] = coefs
        lifted = dot(coefs, vin[...]).astype(BF16)
        src[1] = lifted[:, :R]
        src[2] = lifted[:, R:]
        for j in (4, 5, 3, 6, 2, 7, 1):
            remote(src.at[meet(j)], dst.at[j], send, recv, yflip(j)).start()

    def from_siblings(dst, send, recv):
        remote(dst.at[pl.ds(1, 7)], dst.at[pl.ds(1, 7)], send, recv, mate).wait_recv()
        inner = dot(dst[1], rin[0:R, :])
        pair = dst[2].astype(F32) + dst[3].astype(F32)
        inner = inner + dot(pair.astype(BF16), rin[R:2 * R, :])
        quad = jnp.sum(dst[4:8].astype(F32), axis=0)
        return (inner + dot(quad.astype(BF16), rin[2 * R:3 * R, :])).astype(BF16)

    def scaled(k, value, factor):
        value = value * factor
        twice = jnp.where(k == 2, factor, 1.0)
        return value * twice * twice

    def siblings_start(k):
        g2 = dot(op_s[0], emat[0])
        for leaf in range(1, 4):
            g2 = g2 + dot(op_s[leaf], emat[leaf])
        to_siblings(g2.astype(BF16), sb.at[k], db.at[k], ss.at[3, k], rs.at[3, k])

    def chip_do():
        near = chip_part([op_s[leaf] for leaf in range(4)])
        for leaf in range(4):
            near_s[leaf] = near[leaf]

    def siblings_end(k):
        inner = from_siblings(db.at[k], ss.at[3, k], rs.at[3, k])
        for leaf in range(4):
            near_s[leaf] += dot(inner, emat_t[leaf])

    def ahead_start(k):
        ahead = dot(near_s[0].astype(BF16), efive[0])
        for leaf in range(1, 4):
            ahead = ahead + dot(near_s[leaf].astype(BF16), efive[leaf])
        s1[k + 1] = pack(ahead)
        to_group(k + 1)

    def from_far(k):
        remote(d2.at[k, pl.ds(1, 31)], d2.at[k, pl.ds(1, 31)], ss.at[1, k], rs.at[1, k], mate).wait_recv()
        got = [unpack(d2[k, 1].astype(F32)[None])]
        for level in range(1, 5):
            got.append(unpack(jnp.sum(d2[k, 2**level:2 ** (level + 1)].astype(F32), axis=0)[None]))
        f5 = scaled(k, dot(padded(jnp.concatenate(got, axis=1)), rout[...])[:8], sig_here[:, 0:1])
        s3[k] = pack(f5)[0]
        for j in (4, 5, 3, 6, 2, 7, 1):
            remote(s3.at[k], d3.at[k, ypos], ss.at[2, k], rs.at[2, k], yflip(j)).start()
        d3[k, ypos] = s3[k]
        return f5

    def next_vector(k):
        remote(d3.at[k, pl.ds(1, 7)], d3.at[k, pl.ds(1, 7)], ss.at[2, k], rs.at[2, k], mate).wait_recv()
        far = unpack(d3[k].astype(F32)).astype(BF16)
        for leaf in range(4):
            value = scaled(k, near_s[leaf], sig[:, 0:1]) + dot(far, efive_t[leaf])
            ks[k + 1, leaf] = value * (1.0 / SCALE)
            op_s[leaf] = value.astype(BF16)

    def fed_back(f5):
        return dot(padded(f5), hd2[...].reshape(R, R))[:8]

    def two(p, carry):
        k = 2 * p
        siblings_start(k)

        @pl.when(p == 0)
        def _():
            compose_rest()

        chip_do()
        node = from_group(k)

        @pl.when(p == 0)
        def _():
            to_far(k, node)
            compose_last()
            remote(hd1.at[pl.ds(1, 7)], hd1.at[pl.ds(1, 7)], xs_sem.at[7], xr_sem.at[7], mate).wait_recv()
            part = hs[core, ypos].astype(F32) + jnp.sum(hd1[1:8].astype(F32), axis=0)
            hd2[core, ypos] = part.astype(BF16)
            for j in (4, 5, 3, 6, 2, 7, 1):
                here = hd2.at[core, ypos]
                remote(here, here, xs_sem.at[8], xr_sem.at[8], yflip(j)).start()

        @pl.when(p == 1)
        def _():
            to_far(k, node + fed_back(gs[...]))

        siblings_end(k)
        ahead_start(k)

        @pl.when(p == 0)
        def _():
            rest = hd1.at[pl.ds(1, 7)]
            remote(rest, rest, xs_sem.at[8], xr_sem.at[8], mate).wait_recv()
            remote(hd2.at[core], hd2.at[core], xs_sem.at[10], xr_sem.at[10], mate).start()

        @pl.when(p == 1)
        def _():
            total = sums_end(0)
            after = place(total, 1)
            grown = after > 0.0
            value = jnp.sqrt(total / jnp.where(grown, after, 1.0))
            value = jnp.where(grown, jnp.clip(value, 2.0**-60, 2.0**60), 1.0)
            sig[...] = jnp.broadcast_to(by_column(value), (HALF, 128))
            mine = jnp.sum(jnp.where(lane == ypos, value, 0.0), axis=1, keepdims=True)
            sig_here[...] = jnp.broadcast_to(mine, (8, 128))

        f5 = from_far(k)

        @pl.when(p == 0)
        def _():
            remote(hd2.at[core], hd2.at[core], xs_sem.at[10], xr_sem.at[10], mate).wait_recv()

        to_far(k + 1, scaled(k, from_group(k + 1), sig_here[:, 0:1]) + fed_back(f5))
        next_vector(k)
        k = 2 * p + 1
        siblings_start(k)

        @pl.when(p == 0)
        def _():
            sums_start(0, inner_products(((0, 0, 0), (1, 1, 1)), jnp.zeros((8, 128), F32)))

        chip_do()
        f5 = from_far(k)
        gs[...] = f5

        @pl.when(p == 1)
        def _():
            factor = sig[:, 0:1]
            for leaf in range(4):
                ks[1, leaf] = ks[1, leaf] * factor
                ks[2, leaf] = ks[2, leaf] * factor * factor
            gt[...] = inner_products(EARLY, jnp.zeros((8, 128), F32))

        siblings_end(k)

        @pl.when(p == 0)
        def _():
            ahead_start(k)
            sums_middle(0)

        next_vector(k)
        return carry

    lax.fori_loop(0, ITERS // 2, two, 0)

    sums_start(1, inner_products(LATE, gt[...]))
    sums_middle(1)
    total = sums_end(1)
    table = {}
    for m, left, right in EARLY + LATE:
        table[left, right] = table[right, left] = place(total, m)
    sigma = sig[:, 0:1]
    square = jnp.concatenate([sigma[8 * a:8 * a + 8] for a in range(8)] + [jnp.ones((8, 120), F32)], axis=1)
    rest = 1e-06 * square * square
    left_over = [jnp.ones((8, 128), F32)]
    gained = [jnp.zeros((8, 128), F32) for _ in range(ITERS)]
    for k in range(ITERS):
        num = jnp.zeros((8, 128), F32)
        den = jnp.zeros((8, 128), F32)
        for i in range(k + 1):
            for j in range(k + 1):
                both = left_over[i] * left_over[j]
                num = num + both * table[i, j + 1]
                den = den + both * table[i + 1, j + 1]
        step = num / (den + rest)
        for i in range(k + 1):
            gained[i] = gained[i] + step * left_over[i]
        new = left_over + [jnp.zeros((8, 128), F32)]
        for i in range(k + 1):
            new[i + 1] = new[i + 1] - step * left_over[i]
        left_over = new
    gained = [by_column(value) * sigma for value in gained]
    left_over = [by_column(value) for value in left_over[1:]]

    def outcome(leaf):
        solved = gained[0] * ks[0, leaf]
        residual = ks[0, leaf]
        for i in range(1, ITERS):
            solved = solved + gained[i] * ks[i, leaf]
        for i in range(1, ITERS + 1):
            residual = residual + left_over[i - 1] * ks[i, leaf]
        return solved.astype(BF16), residual.astype(BF16)

    for leaf in range(2):
        otheirs[0, leaf], otheirs[1, leaf] = outcome(2 * (1 - core) + leaf)
    swap = remote(otheirs, omine.at[core], xs_sem.at[6], xr_sem.at[6], mate)
    swap.start()
    for leaf in range(2):
        omine[core, 0, leaf], omine[core, 1, leaf] = outcome(2 * core + leaf)
    sums_sent(0)
    sums_sent(1)
    for earlier in swaps:
        earlier.wait_send()
    rest = hd1.at[pl.ds(1, 7)]
    remote(rest, rest, xs_sem.at[7], xr_sem.at[7], mate).wait_send()
    remote(rest, rest, xs_sem.at[8], xr_sem.at[8], mate).wait_send()
    remote(hd2.at[core], hd2.at[core], xs_sem.at[10], xr_sem.at[10], mate).wait_send()
    for k in range(ITERS):
        remote(s1.at[k, pl.ds(1, 7)], s1.at[k, pl.ds(1, 7)], ss.at[0, k], rs.at[0, k], mate).wait_send()
        remote(d2.at[k, pl.ds(1, 31)], d2.at[k, pl.ds(1, 31)], ss.at[1, k], rs.at[1, k], mate).wait_send()
        remote(d3.at[k, pl.ds(1, 7)], d3.at[k, pl.ds(1, 7)], ss.at[2, k], rs.at[2, k], mate).wait_send()
        remote(db.at[k, pl.ds(1, 7)], db.at[k, pl.ds(1, 7)], ss.at[3, k], rs.at[3, k], mate).wait_send()
    swap.wait_recv()
    writes = []
    for which, out in ((0, out_a), (1, out_b)):
        for leaf in range(2):
            both = jnp.concatenate([omine[0, which, leaf], omine[1, which, leaf]], axis=0)
            outs_v[which, leaf * LEAF:(leaf + 1) * LEAF, :] = both.astype(F32).T.astype(BF16)
        write = pltpu.make_async_copy(outs_v.at[which], out, load_sem.at[which])
        write.start()
        writes.append(write)
    for write in writes:
        write.wait()
    swap.wait_send()


def per_device(rhs, diag_blocks, leaf_bases, leaf_up, chain_up, chain_pair, node_ranks):
    anywhere = pl.BlockSpec(memory_space=pl.ANY)
    vm = pltpu.VMEM
    dma = pltpu.SemaphoreType.DMA
    n = ITERS
    return pl.pallas_call(
        kernel,
        out_shape=(jax.ShapeDtypeStruct((2 * LEAF, 2 * HALF), BF16),) * 2,
        in_specs=[anywhere] * 6 + [pl.BlockSpec(memory_space=pltpu.SMEM)],
        out_specs=(anywhere, anywhere),
        scratch_shapes=[
            vm((2 * LEAF, 2 * HALF), BF16),
            vm((4, LEAF, LEAF), BF16),
            vm((2, LEAF, R), BF16),
            vm((2, R, R), BF16),
            vm((4, LEAF, R), BF16),
            vm((4, R, R), BF16),
            vm((2, R, R), BF16),
            vm((4, R, R), BF16),
            vm((2, R, R), BF16),
            vm((8, R, R), BF16),
            vm((10, R, R), BF16),
            vm((2, 2, HALF, LEAF), BF16),
            vm((4, HALF, LEAF), BF16),
            vm((4, R, LEAF), BF16),
            vm((4, R, R), BF16),
            vm((2, R, R), BF16),
            vm((R, R), BF16),
            vm((4, LEAF, R), BF16),
            vm((4, R, LEAF), BF16),
            vm((4, LEAF, R), BF16),
            vm((4, R, LEAF), BF16),
            vm((R, 2 * R), BF16),
            vm((3 * R, R), BF16),
            vm((R, 4 * R), BF16),
            vm((5 * R, R), BF16),
            vm((n + 1, 4, HALF, LEAF), F32),
            vm((4, HALF, LEAF), BF16),
            vm((4, HALF, LEAF), F32),
            vm((HALF, 128), F32),
            vm((8, 128), F32),
            vm((8, 128), F32),
            vm((n, 8, 16, 128), BF16),
            vm((n, 8, 16, 128), BF16),
            vm((n, 5, 16, 128), BF16),
            vm((n, 32, 16, 128), BF16),
            vm((n, 16, 128), BF16),
            vm((n, 8, 16, 128), BF16),
            vm((n, 3, HALF, R), BF16),
            vm((n, 8, HALF, R), BF16),
            vm((2, 8, 128), F32),
            vm((2, 8, 8, 128), F32),
            vm((2, 32, 8, 128), F32),
            vm((2, 8, 128), F32),
            vm((2, 8, 16, R), BF16),
            vm((8, 16, R), BF16),
            vm((2, 8, 16, R), BF16),
            vm((8, R), F32),
            vm((2, 2, 2, HALF, LEAF), BF16),
            vm((2, 2, HALF, LEAF), BF16),
            vm((2, 2 * LEAF, 2 * HALF), BF16),
            dma((7,)),
            dma((11,)),
            dma((11,)),
            dma((6, n)),
            dma((6, n)),
        ],
        compiler_params=pltpu.CompilerParams(
            collective_id=0, has_side_effects=True, vmem_limit_bytes=56 * 2**20
        ),
        name="sweeps",
    )(rhs, diag_blocks, leaf_bases, leaf_up, chain_up, chain_pair, node_ranks)


def solution(mesh):
    return jax.shard_map(
        per_device,
        mesh=mesh,
        in_specs=(
            P("leaf", None),
            P("leaf", None, None),
            P("leaf", None, None),
            P("leaf", None, None),
            P("leaf", None, None, None),
            P("leaf", None, None, None),
            P("leaf", None),
        ),
        out_specs=(P("leaf", None), P("leaf", None)),
        check_vma=False,
    )
```

```python
import jax
import jax.numpy as jnp
from jax import lax
from jax.experimental import pallas as pl
from jax.experimental.pallas import tpu as pltpu
from jax.sharding import PartitionSpec as P

ITERS = 4
LEAF = 512
R = 256
HALF = 64
SCALE = 2.0**-60
MESH = pl.DeviceIdType.MESH
F32 = jnp.float32
BF16 = jnp.bfloat16
FAR = sorted(range(1, 32), key=lambda j: -(2 * min(j // 8, 2) + min(j % 8, 4)))


PAIRS = [(i, j) for j in range(1, ITERS + 1) for i in range(j + 1)]
EARLY = [(m, i, j) for m, (i, j) in enumerate(PAIRS) if j < ITERS]
LATE = [(m, i, j) for m, (i, j) in enumerate(PAIRS) if j == ITERS]


def meet(offset):
    return offset.bit_length() - 1


def flipped(index, offset):
    bit = 0
    out = index
    while offset >> bit:
        if offset >> bit & 1:
            out = out + (1 - 2 * ((index // 2**bit) % 2)) * 2**bit
        bit += 1
    return out


def dot(left, right):
    return jnp.dot(left, right, preferred_element_type=F32)


def dot_t(left, right):
    return lax.dot_general(left, right, (((1,), (1,)), ((), ())), preferred_element_type=F32)


def flip(matrix):
    return matrix.astype(F32).T.astype(BF16)


def pack(rows):
    count = rows.shape[0] // 8
    low = rows[:, :128].reshape(count, 8, 128)
    high = rows[:, 128:].reshape(count, 8, 128)
    return jnp.concatenate([low, high], axis=1).astype(BF16)


def unpack(tiles):
    count = tiles.shape[0]
    low = tiles[:, :8].reshape(8 * count, 128)
    high = tiles[:, 8:].reshape(8 * count, 128)
    return jnp.concatenate([low, high], axis=1)


def padded(rows):
    return jnp.concatenate([rows, jnp.zeros_like(rows)], axis=0).astype(BF16)


def kernel(
    rhs, diag, bases, lup, cup, cpair, ranks, out_a, out_b,
    rhs_v, diag_v, raw_b, raw_l, bas, lu, w1, p0, cu, cp, xhalf, xin,
    bas_t, lu_t, p0_t, p1_t, emat, emat_t, efour, efour_t, vin, rin, serve, rout, w4, hmat, p4, emix_t, rmix, pre, vout, s1x, d1x,
    ks, op_s, near_s, sig, sig_here, gt,
    s1, d1, s2, d2, s3, d3, sb, db, sa, da1, da2, sa2, hs, hd1, hd2, gs, omine, otheirs, outs_v, gn,
    load_sem, xs_sem, xr_sem, ss, rs,
):
    me = lax.axis_index("leaf")
    core = me % 2
    ypos = (me // 2) % 8
    quad = ypos // 4
    group = me // 16
    mate = me + 1 - 2 * core

    def yflip(j):
        return me + (flipped(ypos, j) - ypos) * 2

    def gflip(j):
        return me + (flipped(group, j) - group) * 16

    own2 = pl.ds(2 * core, 2)
    loads = [
        pltpu.make_async_copy(rhs, rhs_v, load_sem.at[0]),
        pltpu.make_async_copy(bases, raw_b, load_sem.at[1]),
        pltpu.make_async_copy(lup, raw_l, load_sem.at[2]),
        pltpu.make_async_copy(cup.at[0], cu, load_sem.at[3]),
        pltpu.make_async_copy(cpair.at[0], cp, load_sem.at[4]),
        pltpu.make_async_copy(diag, diag_v.at[own2], load_sem.at[5]),
    ]
    for load in loads:
        load.start()

    barrier = pltpu.get_barrier_semaphore()
    peers = [gflip(j) for j in FAR] + [yflip(j) for j in (4, 5, 3, 6, 2, 7, 1)] + [mate]
    for peer in peers:
        pl.semaphore_signal(barrier, inc=1, device_id=(peer,), device_id_type=MESH)

    def remote(src, dst, send, recv, target):
        return pltpu.make_async_remote_copy(
            src_ref=src, dst_ref=dst, send_sem=send, recv_sem=recv, device_id=(target,), device_id_type=MESH
        )

    lanes_w = lax.broadcasted_iota(jnp.int32, (R, R), 1)
    lanes_b = lax.broadcasted_iota(jnp.int32, (LEAF, R), 1)

    def masked(value, lanes, rank):
        return jnp.where(lanes < rank, value.astype(F32), 0.0).astype(BF16)

    def transfer(level):
        return masked(cu[level - 1], lanes_w, ranks[0, level + 2])

    def oriented(level):
        left = (me // 2 ** (level - 1)) % 2 == 0
        return jnp.where(left, cp[level].astype(F32).T, cp[level].astype(F32)).astype(BF16)

    loads[0].wait()
    turned = rhs_v[...].astype(F32).T.astype(BF16)
    for half in range(2):
        for leaf in range(2):
            xhalf[half, leaf] = turned[half * HALF:(half + 1) * HALF, leaf * LEAF:(leaf + 1) * LEAF]
    xin[own2] = xhalf[core]
    loads[1].wait()
    for leaf in range(2):
        bas[2 * core + leaf] = masked(raw_b[leaf], lanes_b, ranks[0, leaf])
    loads[2].wait()
    for leaf in range(2):
        lu[2 * core + leaf] = masked(raw_l[leaf], lanes_w, ranks[0, 2])
    loads[3].wait()
    w1[core] = masked(cu[0], lanes_w, ranks[0, 3])
    loads[4].wait()
    p0[core] = cp[0]
    loads[5].wait()
    vin[...] = transfer(2)
    v4 = dot(vin[...], transfer(3)).astype(BF16)

    def compose(leaf, dev):
        low = dot(lu[leaf], w1[dev]).astype(BF16)
        emat[leaf] = dot(bas[leaf], low).astype(BF16)
        efour[leaf] = dot(bas[leaf], dot(low, v4).astype(BF16)).astype(BF16)

    for leaf in range(2):
        compose(2 * core + leaf, core)

    pl.semaphore_wait(barrier, len(peers))
    own1 = pl.ds(core, 1)
    shared = [(bas, own2), (lu, own2), (w1, own1), (p0, own1), (diag_v, own2)]
    swaps = [remote(xhalf.at[1 - core], xin.at[own2], xs_sem.at[0], xr_sem.at[0], mate)]
    for m, (ref, part) in enumerate(shared):
        swaps.append(remote(ref.at[part], ref.at[part], xs_sem.at[m + 1], xr_sem.at[m + 1], mate))
    for swap in swaps:
        swap.start()
    swaps[0].wait_recv()
    first = xin[...].astype(F32)
    ks[0] = first
    sig[...] = jnp.ones_like(sig)
    sig_here[...] = jnp.ones_like(sig_here)
    op_s[...] = (first * SCALE).astype(BF16)
    for swap in swaps[1:4]:
        swap.wait_recv()
    for leaf in range(2):
        compose(2 * (1 - core) + leaf, 1 - core)

    def to_group(k):
        for j in (4, 5, 3, 6, 2, 7, 1):
            remote(s1.at[k, flipped(ypos, j)], d1.at[k, j], ss.at[0, k], rs.at[0, k], yflip(j)).start()

    def from_group(k):
        remote(d1.at[k, pl.ds(1, 7)], d1.at[k, pl.ds(1, 7)], ss.at[0, k], rs.at[0, k], mate).wait_recv()
        own = s1[k, ypos].astype(F32) + jnp.sum(d1[k, 1:4].astype(F32), axis=0)
        other = jnp.sum(d1[k, 4:8].astype(F32), axis=0)
        return jnp.concatenate([unpack(own[None]), unpack(other[None])], axis=1)

    def far_start(k, lifted):
        for level in range(5):
            s2[k, level] = pack(lifted[:, level * R:(level + 1) * R])[0]
        for j in FAR:
            remote(s2.at[k, meet(j)], d2.at[k, j], ss.at[1, k], rs.at[1, k], gflip(j)).start()

    def quad_pair(node):
        gn[...] = jnp.concatenate([dot(node[:, R:], p4[0]), dot(node[:, :R], p4[1])], axis=1)[:8]

    def to_far(k, node):
        node = padded(node)
        far_start(k, dot(node, serve[...])[:8])
        quad_pair(node)

    g4 = dot(op_s[0], efour[0])
    for leaf in range(1, 4):
        g4 = g4 + dot(op_s[leaf], efour[leaf])
    s1[0] = pack(g4)
    to_group(0)
    s1x[...] = pack(dot(g4.astype(BF16), transfer(4)))
    for j in (4, 5, 3, 6, 2, 7, 1):
        remote(s1x.at[flipped(ypos, j)], d1x.at[j], xs_sem.at[11], xr_sem.at[11], yflip(j)).start()

    half_rows = pl.ds(pl.multiple_of(core * 128, 128), 128)
    lift4 = remote(cup.at[0, 3, half_rows], w4.at[1, core], xs_sem.at[9], xr_sem.at[9], yflip(7))
    lift_swap = remote(w4.at[1, core], w4.at[1, core], xs_sem.at[12], xr_sem.at[12], mate)

    def compose_first():
        for leaf in range(4):
            efour_t[leaf] = flip(efour[leaf])
        gram = dot(efour_t[0], efour[0])
        for leaf in range(1, 4):
            gram = gram + dot(efour_t[leaf], efour[leaf])
        hs[...] = gram.astype(BF16).reshape(2, 8, 16, R)
        for j in (4, 5, 3, 6, 2, 7, 1):
            remote(hs.at[core, flipped(ypos, j)], hd1.at[j], xs_sem.at[7], xr_sem.at[7], yflip(j)).start()
        lift4.start()
        t = transfer(5)
        vout[:, 0:R] = t
        for level in range(6, 9):
            t = dot(t, transfer(level)).astype(BF16)
            vout[:, (level - 5) * R:(level - 4) * R] = t
        p4[0] = oriented(4)
        p4[1] = flip(p4[0])
        for leaf in range(4):
            emat_t[leaf] = flip(emat[leaf])
        rin[0:R, :] = oriented(2)
        rin[R:2 * R, :] = dot_t(oriented(3), vin[...]).astype(BF16)
        mix = dot(emat_t[0], efour[0])
        for leaf in range(1, 4):
            mix = mix + dot(emat_t[leaf], efour[leaf])
        mix = mix.astype(BF16)
        emix_t[...] = flip(mix)
        rmix[...] = dot(rin[...], mix).astype(BF16)
        p1_t[...] = flip(cp[1])
        for swap in swaps[4:]:
            swap.wait_recv()
        for dev in range(2):
            p0_t[dev] = flip(p0[dev])
        for leaf in range(4):
            bas_t[leaf] = flip(bas[leaf])
            lu_t[leaf] = flip(lu[leaf])

    def compose_last():
        lift_swap.wait_recv()
        other = masked(w4[1].reshape(R, R), lanes_w, ranks[0, 6])
        for q, value in ((0, transfer(4)), (1, other)):
            serve[q * R:(q + 1) * R, 0:R] = value
            serve[q * R:(q + 1) * R, R:] = dot(value, vout[...]).astype(BF16)
        for level in range(5, 10):
            at = (level - 5) * R
            turn = oriented(level)
            for q in range(2):
                rout[at:at + R, q * R:(q + 1) * R] = dot_t(turn, serve[q * R:(q + 1) * R, at:at + R]).astype(BF16)

    lane = lax.broadcasted_iota(jnp.int32, (8, 128), 1)

    def inner_products(pairs, tile):
        for m, left, right in pairs:
            got = ks[left, 0] * ks[right, 0]
            for leaf in range(1, 4):
                got = got + ks[left, leaf] * ks[right, leaf]
            got = jnp.sum(got, axis=1, keepdims=True)
            for a in range(8):
                tile = jnp.where(lane == 8 * m + a, got[8 * a:8 * a + 8], tile)
        return tile

    def sums_start(q, tile):
        sa[q] = tile
        for j in (4, 5, 3, 6, 2, 7, 1):
            remote(sa.at[q], da1.at[q, j], ss.at[4, q], rs.at[4, q], yflip(j)).start()

    def sums_middle(q):
        remote(da1.at[q, pl.ds(1, 7)], da1.at[q, pl.ds(1, 7)], ss.at[4, q], rs.at[4, q], mate).wait_recv()
        sa2[q] = sa[q] + jnp.sum(da1[q, 1:8], axis=0)
        for j in FAR:
            remote(sa2.at[q], da2.at[q, j], ss.at[5, q], rs.at[5, q], gflip(j)).start()

    def sums_end(q):
        remote(da2.at[q, pl.ds(1, 31)], da2.at[q, pl.ds(1, 31)], ss.at[5, q], rs.at[5, q], mate).wait_recv()
        return sa2[q] + jnp.sum(da2[q, 1:32], axis=0)

    def sums_sent(q):
        remote(da1.at[q, pl.ds(1, 7)], da1.at[q, pl.ds(1, 7)], ss.at[4, q], rs.at[4, q], mate).wait_send()
        remote(da2.at[q, pl.ds(1, 31)], da2.at[q, pl.ds(1, 31)], ss.at[5, q], rs.at[5, q], mate).wait_send()

    def place(tile, m):
        return tile if m == 0 else pltpu.roll(tile, 128 - 8 * m, 1)

    def by_column(tile):
        return jnp.concatenate([tile[:, a:a + 1] for a in range(8)], axis=0)

    def chip_part(x):
        g_leaf = [dot(x[leaf], bas[leaf]).astype(BF16) for leaf in range(4)]
        g_one = [
            (dot(g_leaf[2 * dev], lu[2 * dev]) + dot(g_leaf[2 * dev + 1], lu[2 * dev + 1])).astype(BF16)
            for dev in range(2)
        ]
        c_one = [dot(g_one[1], p1_t[...]).astype(BF16), dot(g_one[0], cp[1]).astype(BF16)]
        out = []
        for dev in range(2):
            a, b = 2 * dev, 2 * dev + 1
            f_a = dot(g_leaf[b], p0_t[dev]) + dot(c_one[dev], lu_t[a])
            f_b = dot(g_leaf[a], p0[dev]) + dot(c_one[dev], lu_t[b])
            out.append(dot(x[a], diag_v[a]) + dot(f_a.astype(BF16), bas_t[a]))
            out.append(dot(x[b], diag_v[b]) + dot(f_b.astype(BF16), bas_t[b]))
        return out

    def to_siblings(k, coefs):
        coefs = coefs.astype(BF16)
        sb[k, 0] = coefs
        sb[k, 1] = dot(coefs, vin[...]).astype(BF16)
        for j in (3, 2, 1):
            remote(sb.at[k, meet(j)], db.at[k, j], ss.at[3, k], rs.at[3, k], yflip(j)).start()

    def from_siblings(k):
        here = db.at[k, pl.ds(1, 3)]
        remote(here, here, ss.at[3, k], rs.at[3, k], mate).wait_recv()
        pair = db[k, 2].astype(F32) + db[k, 3].astype(F32)
        return jnp.concatenate([db[k, 1], pair.astype(BF16)], axis=1)

    def scaled(k, value, factor):
        value = value * factor
        twice = jnp.where(k == 2, factor, 1.0)
        return value * twice * twice

    def over_leaves(x, matrix):
        total = dot(x[0].astype(BF16), matrix[0])
        for leaf in range(1, 4):
            total = total + dot(x[leaf].astype(BF16), matrix[leaf])
        return total

    def chip_do(look):
        near = chip_part([op_s[leaf] for leaf in range(4)])
        for leaf in range(4):
            near_s[leaf] = near[leaf]
        if look:
            pre[...] = over_leaves(near, efour)

    def siblings_end(k, look):
        coefs = from_siblings(k)
        if look:
            s1[k + 1] = pack(pre[...] + dot(coefs, rmix[...]))
            to_group(k + 1)
        inner = dot(coefs, rin[...]).astype(BF16)
        for leaf in range(4):
            near_s[leaf] += dot(inner, emat_t[leaf])

    def from_far(k):
        remote(d2.at[k, pl.ds(1, 31)], d2.at[k, pl.ds(1, 31)], ss.at[1, k], rs.at[1, k], mate).wait_recv()
        got = [unpack(d2[k, 1].astype(F32)[None])]
        for level in range(1, 5):
            got.append(unpack(jnp.sum(d2[k, 2**level:2 ** (level + 1)].astype(F32), axis=0)[None]))
        f4 = scaled(k, dot(padded(jnp.concatenate(got, axis=1)), rout[...])[:8] + gn[...], sig_here[:, 0:1])
        s3[k, 0] = pack(f4[:, :R])[0]
        s3[k, 1] = pack(f4[:, R:])[0]
        for j in (4, 5, 3, 6, 2, 7, 1):
            remote(s3.at[k, j // 4], d3.at[k, ypos], ss.at[2, k], rs.at[2, k], yflip(j)).start()
        d3[k, ypos] = s3[k, 0]
        return f4

    def next_vector(k, go_on):
        factor = sig[:, 0:1]
        near = [scaled(k, near_s[leaf], factor) for leaf in range(4)]
        if go_on:
            coefs = over_leaves(near, emat)
        for leaf in range(4):
            near_s[leaf] = near[leaf]
        remote(d3.at[k, pl.ds(1, 7)], d3.at[k, pl.ds(1, 7)], ss.at[2, k], rs.at[2, k], mate).wait_recv()
        far = unpack(d3[k].astype(F32)).astype(BF16)
        if go_on:
            to_siblings(k + 1, coefs + dot(far, emix_t[...]))
        for leaf in range(4):
            value = near_s[leaf] + dot(far, efour_t[leaf])
            ks[k + 1, leaf] = value * (1.0 / SCALE)
            op_s[leaf] = value.astype(BF16)

    def fed_back(f4):
        f4 = padded(f4)
        return jnp.concatenate([dot(f4[:, :R], hmat[0]), dot(f4[:, R:], hmat[1])], axis=1)[:8]

    def two(p, carry):
        k = 2 * p

        @pl.when(p == 0)
        def _():
            compose_first()

        chip_do(True)

        @pl.when(p == 0)
        def _():
            rest = d1x.at[pl.ds(1, 7)]
            remote(rest, rest, xs_sem.at[11], xr_sem.at[11], mate).wait_recv()
            ring = unpack((s1x[ypos].astype(F32) + jnp.sum(d1x[1:8].astype(F32), axis=0))[None])
            far_start(k, jnp.concatenate([ring, dot(padded(ring), vout[...])[:8]], axis=1))
            quad_pair(padded(from_group(k)))

        @pl.when(p == 1)
        def _():
            back = fed_back(gs[...])
            to_far(k, back + from_group(k))

        siblings_end(k, True)

        @pl.when(p == 0)
        def _():
            remote(hd1.at[pl.ds(1, 7)], hd1.at[pl.ds(1, 7)], xs_sem.at[7], xr_sem.at[7], mate).wait_recv()
            part = hs[core, ypos].astype(F32) + jnp.sum(hd1[1:4].astype(F32), axis=0)
            hd2[core, ypos, quad] = part.astype(BF16)
            hd2[core, ypos, 1 - quad] = jnp.sum(hd1[4:8].astype(F32), axis=0).astype(BF16)
            for j in (4, 5, 3, 6, 2, 7, 1):
                here = hd2.at[core, ypos]
                remote(here, here, xs_sem.at[8], xr_sem.at[8], yflip(j)).start()
            lift4.wait_recv()
            lift_swap.start()
            compose_last()
            rest = hd2.at[core, pl.ds(1, 7)]
            remote(rest, rest, xs_sem.at[8], xr_sem.at[8], mate).wait_recv()
            remote(hd2.at[core], hd2.at[core], xs_sem.at[10], xr_sem.at[10], mate).start()

        @pl.when(p == 1)
        def _():
            total = sums_end(0)
            after = place(total, 1)
            grown = after > 0.0
            value = jnp.sqrt(total / jnp.where(grown, after, 1.0))
            value = jnp.where(grown, jnp.clip(value, 2.0**-60, 2.0**60), 1.0)
            sig[...] = jnp.broadcast_to(by_column(value), (HALF, 128))
            mine = jnp.sum(jnp.where(lane == ypos, value, 0.0), axis=1, keepdims=True)
            sig_here[...] = jnp.broadcast_to(mine, (8, 128))

        f4 = from_far(k)

        @pl.when(p == 0)
        def _():
            remote(hd2.at[core], hd2.at[core], xs_sem.at[10], xr_sem.at[10], mate).wait_recv()
            halves = [hd2[:, :, q].reshape(R, R) for q in range(2)]
            hmat[0] = jnp.where(quad == 0, halves[0], halves[1])
            hmat[1] = jnp.where(quad == 0, halves[1], halves[0])

        back = fed_back(f4)
        to_far(k + 1, back + scaled(k, from_group(k + 1), sig_here[:, 0:1]))
        next_vector(k, True)
        k = 2 * p + 1

        @pl.when(p == 0)
        def _():
            sums_start(0, inner_products(((0, 0, 0), (1, 1, 1)), jnp.zeros((8, 128), F32)))

        chip_do(True)
        f4 = from_far(k)
        gs[...] = f4

        @pl.when(p == 1)
        def _():
            factor = sig[:, 0:1]
            for leaf in range(4):
                ks[1, leaf] = ks[1, leaf] * factor
                ks[2, leaf] = ks[2, leaf] * factor * factor
            gt[...] = inner_products(EARLY, jnp.zeros((8, 128), F32))

        @pl.when(p == 0)
        def _():
            siblings_end(k, True)
            sums_middle(0)
            next_vector(k, True)

        @pl.when(p == 1)
        def _():
            siblings_end(k, False)
            next_vector(k, False)

        return carry

    to_siblings(0, over_leaves(op_s, emat))
    lax.fori_loop(0, ITERS // 2, two, 0)

    sums_start(1, inner_products(LATE, gt[...]))
    sums_middle(1)
    total = sums_end(1)
    table = {}
    for m, left, right in EARLY + LATE:
        table[left, right] = table[right, left] = place(total, m)
    sigma = sig[:, 0:1]
    square = jnp.concatenate([sigma[8 * a:8 * a + 8] for a in range(8)] + [jnp.ones((8, 120), F32)], axis=1)
    rest = 1e-06 * square * square
    left_over = [jnp.ones((8, 128), F32)]
    gained = [jnp.zeros((8, 128), F32) for _ in range(ITERS)]
    for k in range(ITERS):
        num = jnp.zeros((8, 128), F32)
        den = jnp.zeros((8, 128), F32)
        for i in range(k + 1):
            for j in range(k + 1):
                both = left_over[i] * left_over[j]
                num = num + both * table[i, j + 1]
                den = den + both * table[i + 1, j + 1]
        step = num / (den + rest)
        for i in range(k + 1):
            gained[i] = gained[i] + step * left_over[i]
        new = left_over + [jnp.zeros((8, 128), F32)]
        for i in range(k + 1):
            new[i + 1] = new[i + 1] - step * left_over[i]
        left_over = new
    gained = [by_column(value) * sigma for value in gained]
    left_over = [by_column(value) for value in left_over[1:]]

    def outcome(leaf):
        solved = gained[0] * ks[0, leaf]
        residual = ks[0, leaf]
        for i in range(1, ITERS):
            solved = solved + gained[i] * ks[i, leaf]
        for i in range(1, ITERS + 1):
            residual = residual + left_over[i - 1] * ks[i, leaf]
        return solved.astype(BF16), residual.astype(BF16)

    for leaf in range(2):
        otheirs[0, leaf], otheirs[1, leaf] = outcome(2 * (1 - core) + leaf)
    swap = remote(otheirs, omine.at[core], xs_sem.at[6], xr_sem.at[6], mate)
    swap.start()
    for leaf in range(2):
        omine[core, 0, leaf], omine[core, 1, leaf] = outcome(2 * core + leaf)
    sums_sent(0)
    sums_sent(1)
    for earlier in swaps:
        earlier.wait_send()
    rest = hd1.at[pl.ds(1, 7)]
    remote(rest, rest, xs_sem.at[7], xr_sem.at[7], mate).wait_send()
    rest = hd2.at[core, pl.ds(1, 7)]
    remote(rest, rest, xs_sem.at[8], xr_sem.at[8], mate).wait_send()
    lift4.wait_send()
    lift_swap.wait_send()
    rest = d1x.at[pl.ds(1, 7)]
    remote(rest, rest, xs_sem.at[11], xr_sem.at[11], mate).wait_send()
    remote(hd2.at[core], hd2.at[core], xs_sem.at[10], xr_sem.at[10], mate).wait_send()
    for k in range(ITERS):
        remote(s1.at[k, pl.ds(1, 7)], s1.at[k, pl.ds(1, 7)], ss.at[0, k], rs.at[0, k], mate).wait_send()
        remote(d2.at[k, pl.ds(1, 31)], d2.at[k, pl.ds(1, 31)], ss.at[1, k], rs.at[1, k], mate).wait_send()
        remote(d3.at[k, pl.ds(1, 7)], d3.at[k, pl.ds(1, 7)], ss.at[2, k], rs.at[2, k], mate).wait_send()
        remote(db.at[k, pl.ds(1, 3)], db.at[k, pl.ds(1, 3)], ss.at[3, k], rs.at[3, k], mate).wait_send()
    swap.wait_recv()
    writes = []
    for which, out in ((0, out_a), (1, out_b)):
        for leaf in range(2):
            both = jnp.concatenate([omine[0, which, leaf], omine[1, which, leaf]], axis=0)
            outs_v[which, leaf * LEAF:(leaf + 1) * LEAF, :] = both.astype(F32).T.astype(BF16)
        write = pltpu.make_async_copy(outs_v.at[which], out, load_sem.at[which])
        write.start()
        writes.append(write)
    for write in writes:
        write.wait()
    swap.wait_send()


def per_device(rhs, diag_blocks, leaf_bases, leaf_up, chain_up, chain_pair, node_ranks):
    anywhere = pl.BlockSpec(memory_space=pl.ANY)
    vm = pltpu.VMEM
    dma = pltpu.SemaphoreType.DMA
    n = ITERS
    return pl.pallas_call(
        kernel,
        out_shape=(jax.ShapeDtypeStruct((2 * LEAF, 2 * HALF), BF16),) * 2,
        in_specs=[anywhere] * 6 + [pl.BlockSpec(memory_space=pltpu.SMEM)],
        out_specs=(anywhere, anywhere),
        scratch_shapes=[
            vm((2 * LEAF, 2 * HALF), BF16),
            vm((4, LEAF, LEAF), BF16),
            vm((2, LEAF, R), BF16),
            vm((2, R, R), BF16),
            vm((4, LEAF, R), BF16),
            vm((4, R, R), BF16),
            vm((2, R, R), BF16),
            vm((2, R, R), BF16),
            vm((8, R, R), BF16),
            vm((10, R, R), BF16),
            vm((2, 2, HALF, LEAF), BF16),
            vm((4, HALF, LEAF), BF16),
            vm((4, R, LEAF), BF16),
            vm((4, R, R), BF16),
            vm((2, R, R), BF16),
            vm((R, R), BF16),
            vm((4, LEAF, R), BF16),
            vm((4, R, LEAF), BF16),
            vm((4, LEAF, R), BF16),
            vm((4, R, LEAF), BF16),
            vm((R, R), BF16),
            vm((2 * R, R), BF16),
            vm((2 * R, 5 * R), BF16),
            vm((5 * R, 2 * R), BF16),
            vm((2, 2, 128, R), BF16),
            vm((2, R, R), BF16),
            vm((2, R, R), BF16),
            vm((R, R), BF16),
            vm((2 * R, R), BF16),
            vm((HALF, R), F32),
            vm((R, 4 * R), BF16),
            vm((8, 16, 128), BF16),
            vm((8, 16, 128), BF16),
            vm((n + 1, 4, HALF, LEAF), F32),
            vm((4, HALF, LEAF), BF16),
            vm((4, HALF, LEAF), F32),
            vm((HALF, 128), F32),
            vm((8, 128), F32),
            vm((8, 128), F32),
            vm((n, 8, 16, 128), BF16),
            vm((n, 8, 16, 128), BF16),
            vm((n, 5, 16, 128), BF16),
            vm((n, 32, 16, 128), BF16),
            vm((n, 2, 16, 128), BF16),
            vm((n, 8, 16, 128), BF16),
            vm((n, 2, HALF, R), BF16),
            vm((n, 4, HALF, R), BF16),
            vm((2, 8, 128), F32),
            vm((2, 8, 8, 128), F32),
            vm((2, 32, 8, 128), F32),
            vm((2, 8, 128), F32),
            vm((2, 8, 16, R), BF16),
            vm((8, 16, R), BF16),
            vm((2, 8, 2, 16, R), BF16),
            vm((8, 2 * R), F32),
            vm((2, 2, 2, HALF, LEAF), BF16),
            vm((2, 2, HALF, LEAF), BF16),
            vm((2, 2 * LEAF, 2 * HALF), BF16),
            vm((8, 2 * R), F32),
            dma((7,)),
            dma((13,)),
            dma((13,)),
            dma((6, n)),
            dma((6, n)),
        ],
        compiler_params=pltpu.CompilerParams(
            collective_id=0, has_side_effects=True, vmem_limit_bytes=56 * 2**20
        ),
        name="sweeps",
    )(rhs, diag_blocks, leaf_bases, leaf_up, chain_up, chain_pair, node_ranks)


def solution(mesh):
    return jax.shard_map(
        per_device,
        mesh=mesh,
        in_specs=(
            P("leaf", None),
            P("leaf", None, None),
            P("leaf", None, None),
            P("leaf", None, None),
            P("leaf", None, None, None),
            P("leaf", None, None, None),
            P("leaf", None),
        ),
        out_specs=(P("leaf", None), P("leaf", None)),
        check_vma=False,
    )
```

```python
import jax
import jax.numpy as jnp
from jax import lax
from jax.experimental import pallas as pl
from jax.experimental.pallas import tpu as pltpu
from jax.sharding import PartitionSpec as P

ITERS = 4
LEAF = 512
R = 256
HALF = 64
SCALE = 2.0**-60
MESH = pl.DeviceIdType.MESH
F32 = jnp.float32
BF16 = jnp.bfloat16
FAR = sorted(range(1, 32), key=lambda j: -(2 * min(j // 8, 2) + min(j % 8, 4)))


PAIRS = [(i, j) for j in range(1, ITERS + 1) for i in range(j + 1)]
EARLY = [(m, i, j) for m, (i, j) in enumerate(PAIRS) if j < ITERS]
LATE = [(i, i, j) for i, j in PAIRS if j == ITERS]


def meet(offset):
    return offset.bit_length() - 1


def flipped(index, offset):
    bit = 0
    out = index
    while offset >> bit:
        if offset >> bit & 1:
            out = out + (1 - 2 * ((index // 2**bit) % 2)) * 2**bit
        bit += 1
    return out


def dot(left, right):
    return jnp.dot(left, right, preferred_element_type=F32)


def dot_t(left, right):
    return lax.dot_general(left, right, (((1,), (1,)), ((), ())), preferred_element_type=F32)


def flip(matrix):
    return matrix.astype(F32).T.astype(BF16)


def pack(rows):
    count = rows.shape[0] // 8
    low = rows[:, :128].reshape(count, 8, 128)
    high = rows[:, 128:].reshape(count, 8, 128)
    return jnp.concatenate([low, high], axis=1).astype(BF16)


def unpack(tiles):
    count = tiles.shape[0]
    low = tiles[:, :8].reshape(8 * count, 128)
    high = tiles[:, 8:].reshape(8 * count, 128)
    return jnp.concatenate([low, high], axis=1)


def padded(rows):
    return jnp.concatenate([rows, jnp.zeros_like(rows)], axis=0).astype(BF16)


def kernel(
    rhs, diag, bases, lup, cup, cpair, ranks, out_a, out_b,
    rhs_v, diag_v, raw_b, raw_l, bas, lu, w1, p0, cu, cp, xhalf, xin,
    bas_t, lu_t, p0_t, p1_t, emat, emat_t, efour, efour_t, vin, rin, serve, rout, w4, hmat, p4, emix_t, rmix, pre, vout, s1x, d1x,
    ks, op_s, near_s, sig, sig_here, sl, dl1, dl2, sl2,
    s1, d1, s2, d2, s3, d3, sb, db, sa, da1, da2, sa2, hs, hd1, hd2, gs, omine, otheirs, outs_v, gn,
    load_sem, xs_sem, xr_sem, ss, rs,
):
    me = lax.axis_index("leaf")
    core = me % 2
    ypos = (me // 2) % 8
    quad = ypos // 4
    group = me // 16
    mate = me + 1 - 2 * core

    def yflip(j):
        return me + (flipped(ypos, j) - ypos) * 2

    def gflip(j):
        return me + (flipped(group, j) - group) * 16

    own2 = pl.ds(2 * core, 2)
    loads = [
        pltpu.make_async_copy(rhs, rhs_v, load_sem.at[0]),
        pltpu.make_async_copy(bases, raw_b, load_sem.at[1]),
        pltpu.make_async_copy(lup, raw_l, load_sem.at[2]),
        pltpu.make_async_copy(cup.at[0], cu, load_sem.at[3]),
        pltpu.make_async_copy(cpair.at[0], cp, load_sem.at[4]),
        pltpu.make_async_copy(diag, diag_v.at[own2], load_sem.at[5]),
    ]
    for load in loads:
        load.start()

    barrier = pltpu.get_barrier_semaphore()
    peers = [gflip(j) for j in FAR] + [yflip(j) for j in (4, 5, 3, 6, 2, 7, 1)] + [mate]
    for peer in peers:
        pl.semaphore_signal(barrier, inc=1, device_id=(peer,), device_id_type=MESH)

    def remote(src, dst, send, recv, target):
        return pltpu.make_async_remote_copy(
            src_ref=src, dst_ref=dst, send_sem=send, recv_sem=recv, device_id=(target,), device_id_type=MESH
        )

    lanes_w = lax.broadcasted_iota(jnp.int32, (R, R), 1)
    lanes_b = lax.broadcasted_iota(jnp.int32, (LEAF, R), 1)

    def masked(value, lanes, rank):
        return jnp.where(lanes < rank, value.astype(F32), 0.0).astype(BF16)

    def transfer(level):
        return masked(cu[level - 1], lanes_w, ranks[0, level + 2])

    def oriented(level):
        left = (me // 2 ** (level - 1)) % 2 == 0
        return jnp.where(left, cp[level].astype(F32).T, cp[level].astype(F32)).astype(BF16)

    loads[0].wait()
    turned = rhs_v[...].astype(F32).T.astype(BF16)
    for half in range(2):
        for leaf in range(2):
            xhalf[half, leaf] = turned[half * HALF:(half + 1) * HALF, leaf * LEAF:(leaf + 1) * LEAF]
    xin[own2] = xhalf[core]
    loads[1].wait()
    for leaf in range(2):
        bas[2 * core + leaf] = masked(raw_b[leaf], lanes_b, ranks[0, leaf])
    loads[2].wait()
    for leaf in range(2):
        lu[2 * core + leaf] = masked(raw_l[leaf], lanes_w, ranks[0, 2])
    loads[3].wait()
    w1[core] = masked(cu[0], lanes_w, ranks[0, 3])
    loads[4].wait()
    p0[core] = cp[0]
    loads[5].wait()
    vin[...] = transfer(2)
    v4 = dot(vin[...], transfer(3)).astype(BF16)

    def compose(leaf, dev):
        low = dot(lu[leaf], w1[dev]).astype(BF16)
        emat[leaf] = dot(bas[leaf], low).astype(BF16)
        efour[leaf] = dot(bas[leaf], dot(low, v4).astype(BF16)).astype(BF16)

    for leaf in range(2):
        compose(2 * core + leaf, core)

    pl.semaphore_wait(barrier, len(peers))
    own1 = pl.ds(core, 1)
    shared = [(bas, own2), (lu, own2), (w1, own1), (p0, own1), (diag_v, own2)]
    swaps = [remote(xhalf.at[1 - core], xin.at[own2], xs_sem.at[0], xr_sem.at[0], mate)]
    for m, (ref, part) in enumerate(shared):
        swaps.append(remote(ref.at[part], ref.at[part], xs_sem.at[m + 1], xr_sem.at[m + 1], mate))
    for swap in swaps:
        swap.start()
    swaps[0].wait_recv()
    first = xin[...].astype(F32)
    ks[0] = first
    sig[...] = jnp.ones_like(sig)
    sig_here[...] = jnp.ones_like(sig_here)
    op_s[...] = (first * SCALE).astype(BF16)
    for swap in swaps[1:4]:
        swap.wait_recv()
    for leaf in range(2):
        compose(2 * (1 - core) + leaf, 1 - core)

    def to_group(k):
        for j in (4, 5, 3, 6, 2, 7, 1):
            remote(s1.at[k, flipped(ypos, j)], d1.at[k, j], ss.at[0, k], rs.at[0, k], yflip(j)).start()

    def from_group(k):
        remote(d1.at[k, pl.ds(1, 7)], d1.at[k, pl.ds(1, 7)], ss.at[0, k], rs.at[0, k], mate).wait_recv()
        own = s1[k, ypos].astype(F32) + jnp.sum(d1[k, 1:4].astype(F32), axis=0)
        other = jnp.sum(d1[k, 4:8].astype(F32), axis=0)
        return jnp.concatenate([unpack(own[None]), unpack(other[None])], axis=1)

    def far_start(k, lifted):
        for level in range(5):
            s2[k, level] = pack(lifted[:, level * R:(level + 1) * R])[0]
        for j in FAR:
            remote(s2.at[k, meet(j)], d2.at[k, j], ss.at[1, k], rs.at[1, k], gflip(j)).start()

    def quad_pair(node):
        gn[...] = jnp.concatenate([dot(node[:, R:], p4[0]), dot(node[:, :R], p4[1])], axis=1)[:8]

    def to_far(k, node):
        node = padded(node)
        far_start(k, dot(node, serve[...])[:8])
        quad_pair(node)

    g4 = dot(op_s[0], efour[0])
    for leaf in range(1, 4):
        g4 = g4 + dot(op_s[leaf], efour[leaf])
    s1[0] = pack(g4)
    to_group(0)
    s1x[...] = pack(dot(g4.astype(BF16), transfer(4)))
    for j in (4, 5, 3, 6, 2, 7, 1):
        remote(s1x.at[flipped(ypos, j)], d1x.at[j], xs_sem.at[11], xr_sem.at[11], yflip(j)).start()

    half_rows = pl.ds(pl.multiple_of(core * 128, 128), 128)
    lift4 = remote(cup.at[0, 3, half_rows], w4.at[1, core], xs_sem.at[9], xr_sem.at[9], yflip(7))
    lift_swap = remote(w4.at[1, core], w4.at[1, core], xs_sem.at[12], xr_sem.at[12], mate)

    def compose_first():
        for leaf in range(4):
            efour_t[leaf] = flip(efour[leaf])
        gram = dot(efour_t[0], efour[0])
        for leaf in range(1, 4):
            gram = gram + dot(efour_t[leaf], efour[leaf])
        hs[...] = gram.astype(BF16).reshape(2, 8, 16, R)
        for j in (4, 5, 3, 6, 2, 7, 1):
            remote(hs.at[core, flipped(ypos, j)], hd1.at[j], xs_sem.at[7], xr_sem.at[7], yflip(j)).start()
        lift4.start()
        t = transfer(5)
        vout[:, 0:R] = t
        for level in range(6, 9):
            t = dot(t, transfer(level)).astype(BF16)
            vout[:, (level - 5) * R:(level - 4) * R] = t
        p4[0] = oriented(4)
        p4[1] = flip(p4[0])
        for leaf in range(4):
            emat_t[leaf] = flip(emat[leaf])
        rin[0:R, :] = oriented(2)
        rin[R:2 * R, :] = dot_t(oriented(3), vin[...]).astype(BF16)
        mix = dot(emat_t[0], efour[0])
        for leaf in range(1, 4):
            mix = mix + dot(emat_t[leaf], efour[leaf])
        mix = mix.astype(BF16)
        emix_t[...] = flip(mix)
        rmix[...] = dot(rin[...], mix).astype(BF16)
        p1_t[...] = flip(cp[1])
        for swap in swaps[4:]:
            swap.wait_recv()
        for dev in range(2):
            p0_t[dev] = flip(p0[dev])
        for leaf in range(4):
            bas_t[leaf] = flip(bas[leaf])
            lu_t[leaf] = flip(lu[leaf])

    def compose_last():
        lift_swap.wait_recv()
        other = masked(w4[1].reshape(R, R), lanes_w, ranks[0, 6])
        for q, value in ((0, transfer(4)), (1, other)):
            serve[q * R:(q + 1) * R, 0:R] = value
            serve[q * R:(q + 1) * R, R:] = dot(value, vout[...]).astype(BF16)
        for level in range(5, 10):
            at = (level - 5) * R
            turn = oriented(level)
            for q in range(2):
                rout[at:at + R, q * R:(q + 1) * R] = dot_t(turn, serve[q * R:(q + 1) * R, at:at + R]).astype(BF16)

    lane = lax.broadcasted_iota(jnp.int32, (8, 128), 1)

    def inner_products(pairs, tile):
        for m, left, right in pairs:
            got = ks[left, 0] * ks[right, 0]
            for leaf in range(1, 4):
                got = got + ks[left, leaf] * ks[right, leaf]
            got = jnp.sum(got, axis=1, keepdims=True)
            for a in range(8):
                tile = jnp.where(lane == 8 * m + a, got[8 * a:8 * a + 8], tile)
        return tile

    def of_sums(q):
        return (sl, dl1, dl2, sl2) if q == 2 else (sa.at[q], da1.at[q], da2.at[q], sa2.at[q])

    def sums_start(q, tile):
        mine, near, _, _ = of_sums(q)
        mine[...] = tile
        for j in (4, 5, 3, 6, 2, 7, 1):
            remote(mine, near.at[j], ss.at[4, q], rs.at[4, q], yflip(j)).start()

    def sums_middle(q):
        mine, near, far, total = of_sums(q)
        rest = near.at[pl.ds(1, 7)]
        remote(rest, rest, ss.at[4, q], rs.at[4, q], mate).wait_recv()
        total[...] = mine[...] + jnp.sum(near[1:8], axis=0)
        for j in FAR:
            remote(total, far.at[j], ss.at[5, q], rs.at[5, q], gflip(j)).start()

    def sums_end(q):
        _, _, far, total = of_sums(q)
        rest = far.at[pl.ds(1, 31)]
        remote(rest, rest, ss.at[5, q], rs.at[5, q], mate).wait_recv()
        return total[...] + jnp.sum(far[1:32], axis=0)

    def sums_sent(q):
        _, near, far, _ = of_sums(q)
        rest = near.at[pl.ds(1, 7)]
        remote(rest, rest, ss.at[4, q], rs.at[4, q], mate).wait_send()
        rest = far.at[pl.ds(1, 31)]
        remote(rest, rest, ss.at[5, q], rs.at[5, q], mate).wait_send()

    def place(tile, m):
        return tile if m == 0 else pltpu.roll(tile, 128 - 8 * m, 1)

    def by_column(tile):
        return jnp.concatenate([tile[:, a:a + 1] for a in range(8)], axis=0)

    def chip_part(x):
        g_leaf = [dot(x[leaf], bas[leaf]).astype(BF16) for leaf in range(4)]
        g_one = [
            (dot(g_leaf[2 * dev], lu[2 * dev]) + dot(g_leaf[2 * dev + 1], lu[2 * dev + 1])).astype(BF16)
            for dev in range(2)
        ]
        c_one = [dot(g_one[1], p1_t[...]).astype(BF16), dot(g_one[0], cp[1]).astype(BF16)]
        out = []
        for dev in range(2):
            a, b = 2 * dev, 2 * dev + 1
            f_a = dot(g_leaf[b], p0_t[dev]) + dot(c_one[dev], lu_t[a])
            f_b = dot(g_leaf[a], p0[dev]) + dot(c_one[dev], lu_t[b])
            out.append(dot(x[a], diag_v[a]) + dot(f_a.astype(BF16), bas_t[a]))
            out.append(dot(x[b], diag_v[b]) + dot(f_b.astype(BF16), bas_t[b]))
        return out

    def to_siblings(k, coefs):
        coefs = coefs.astype(BF16)
        sb[k, 0] = coefs
        sb[k, 1] = dot(coefs, vin[...]).astype(BF16)
        for j in (3, 2, 1):
            remote(sb.at[k, meet(j)], db.at[k, j], ss.at[3, k], rs.at[3, k], yflip(j)).start()

    def from_siblings(k):
        here = db.at[k, pl.ds(1, 3)]
        remote(here, here, ss.at[3, k], rs.at[3, k], mate).wait_recv()
        pair = db[k, 2].astype(F32) + db[k, 3].astype(F32)
        return jnp.concatenate([db[k, 1], pair.astype(BF16)], axis=1)

    def scaled(k, value, factor):
        value = value * factor
        twice = jnp.where(k == 2, factor, 1.0)
        return value * twice * twice

    def over_leaves(x, matrix):
        total = dot(x[0].astype(BF16), matrix[0])
        for leaf in range(1, 4):
            total = total + dot(x[leaf].astype(BF16), matrix[leaf])
        return total

    def chip_do(look):
        near = chip_part([op_s[leaf] for leaf in range(4)])
        for leaf in range(4):
            near_s[leaf] = near[leaf]
        if look:
            pre[...] = over_leaves(near, efour)

    def siblings_end(k, look):
        coefs = from_siblings(k)
        if look:
            s1[k + 1] = pack(pre[...] + dot(coefs, rmix[...]))
            to_group(k + 1)
        inner = dot(coefs, rin[...]).astype(BF16)
        for leaf in range(4):
            near_s[leaf] += dot(inner, emat_t[leaf])

    def from_far(k):
        remote(d2.at[k, pl.ds(1, 31)], d2.at[k, pl.ds(1, 31)], ss.at[1, k], rs.at[1, k], mate).wait_recv()
        got = [unpack(d2[k, 1].astype(F32)[None])]
        for level in range(1, 5):
            got.append(unpack(jnp.sum(d2[k, 2**level:2 ** (level + 1)].astype(F32), axis=0)[None]))
        f4 = scaled(k, dot(padded(jnp.concatenate(got, axis=1)), rout[...])[:8] + gn[...], sig_here[:, 0:1])
        s3[k, 0] = pack(f4[:, :R])[0]
        s3[k, 1] = pack(f4[:, R:])[0]
        for j in (4, 5, 3, 6, 2, 7, 1):
            remote(s3.at[k, j // 4], d3.at[k, ypos], ss.at[2, k], rs.at[2, k], yflip(j)).start()
        d3[k, ypos] = s3[k, 0]
        return f4

    def next_vector(k, go_on):
        factor = sig[:, 0:1]
        near = [scaled(k, near_s[leaf], factor) for leaf in range(4)]
        if go_on:
            coefs = over_leaves(near, emat)
        for leaf in range(4):
            near_s[leaf] = near[leaf]
        remote(d3.at[k, pl.ds(1, 7)], d3.at[k, pl.ds(1, 7)], ss.at[2, k], rs.at[2, k], mate).wait_recv()
        far = unpack(d3[k].astype(F32)).astype(BF16)
        if go_on:
            to_siblings(k + 1, coefs + dot(far, emix_t[...]))
        for leaf in range(4):
            value = near_s[leaf] + dot(far, efour_t[leaf])
            ks[k + 1, leaf] = value * (1.0 / SCALE)
            op_s[leaf] = value.astype(BF16)

    def fed_back(f4):
        f4 = padded(f4)
        return jnp.concatenate([dot(f4[:, :R], hmat[0]), dot(f4[:, R:], hmat[1])], axis=1)[:8]

    def two(p, carry):
        k = 2 * p

        @pl.when(p == 0)
        def _():
            compose_first()

        chip_do(True)

        @pl.when(p == 0)
        def _():
            rest = d1x.at[pl.ds(1, 7)]
            remote(rest, rest, xs_sem.at[11], xr_sem.at[11], mate).wait_recv()
            ring = unpack((s1x[ypos].astype(F32) + jnp.sum(d1x[1:8].astype(F32), axis=0))[None])
            far_start(k, jnp.concatenate([ring, dot(padded(ring), vout[...])[:8]], axis=1))
            quad_pair(padded(from_group(k)))

        @pl.when(p == 1)
        def _():
            back = fed_back(gs[...])
            to_far(k, back + from_group(k))

        siblings_end(k, True)

        @pl.when(p == 0)
        def _():
            remote(hd1.at[pl.ds(1, 7)], hd1.at[pl.ds(1, 7)], xs_sem.at[7], xr_sem.at[7], mate).wait_recv()
            part = hs[core, ypos].astype(F32) + jnp.sum(hd1[1:4].astype(F32), axis=0)
            hd2[core, ypos, quad] = part.astype(BF16)
            hd2[core, ypos, 1 - quad] = jnp.sum(hd1[4:8].astype(F32), axis=0).astype(BF16)
            for j in (4, 5, 3, 6, 2, 7, 1):
                here = hd2.at[core, ypos]
                remote(here, here, xs_sem.at[8], xr_sem.at[8], yflip(j)).start()
            lift4.wait_recv()
            lift_swap.start()
            compose_last()
            rest = hd2.at[core, pl.ds(1, 7)]
            remote(rest, rest, xs_sem.at[8], xr_sem.at[8], mate).wait_recv()
            remote(hd2.at[core], hd2.at[core], xs_sem.at[10], xr_sem.at[10], mate).start()

        @pl.when(p == 1)
        def _():
            total = sums_end(0)
            after = place(total, 1)
            grown = after > 0.0
            value = jnp.sqrt(total / jnp.where(grown, after, 1.0))
            value = jnp.where(grown, jnp.clip(value, 2.0**-60, 2.0**60), 1.0)
            sig[...] = jnp.broadcast_to(by_column(value), (HALF, 128))
            mine = jnp.sum(jnp.where(lane == ypos, value, 0.0), axis=1, keepdims=True)
            sig_here[...] = jnp.broadcast_to(mine, (8, 128))

        f4 = from_far(k)

        @pl.when(p == 0)
        def _():
            remote(hd2.at[core], hd2.at[core], xs_sem.at[10], xr_sem.at[10], mate).wait_recv()
            halves = [hd2[:, :, q].reshape(R, R) for q in range(2)]
            hmat[0] = jnp.where(quad == 0, halves[0], halves[1])
            hmat[1] = jnp.where(quad == 0, halves[1], halves[0])

        back = fed_back(f4)
        to_far(k + 1, back + scaled(k, from_group(k + 1), sig_here[:, 0:1]))
        next_vector(k, True)
        k = 2 * p + 1

        @pl.when(p == 0)
        def _():
            sums_start(0, inner_products(((0, 0, 0), (1, 1, 1)), jnp.zeros((8, 128), F32)))

        chip_do(True)
        f4 = from_far(k)
        gs[...] = f4

        @pl.when(p == 1)
        def _():
            factor = sig[:, 0:1]
            for leaf in range(4):
                ks[1, leaf] = ks[1, leaf] * factor
                ks[2, leaf] = ks[2, leaf] * factor * factor
            sums_start(1, inner_products(EARLY, jnp.zeros((8, 128), F32)))

        @pl.when(p == 0)
        def _():
            siblings_end(k, True)
            sums_middle(0)
            next_vector(k, True)

        @pl.when(p == 1)
        def _():
            siblings_end(k, False)
            sums_middle(1)
            next_vector(k, False)

        return carry

    to_siblings(0, over_leaves(op_s, emat))
    lax.fori_loop(0, ITERS // 2, two, 0)

    tile = inner_products(LATE, jnp.zeros((8, 128), F32))
    sums_start(2, tile[0:4] + pltpu.roll(tile, 64, 1)[4:8])
    sums_middle(2)
    total = sums_end(1)
    late = sums_end(2)
    late = jnp.concatenate([late, late], axis=0)
    row = lax.broadcasted_iota(jnp.int32, (8, 128), 0)
    late = jnp.where(row < 4, late, pltpu.roll(late, 64, 1))
    table = {}
    for m, left, right in EARLY + LATE:
        table[left, right] = table[right, left] = place(late if right == ITERS else total, m)
    sigma = sig[:, 0:1]
    square = jnp.concatenate([sigma[8 * a:8 * a + 8] for a in range(8)] + [jnp.ones((8, 120), F32)], axis=1)
    rest = 1e-06 * square * square
    left_over = [jnp.ones((8, 128), F32)]
    gained = [jnp.zeros((8, 128), F32) for _ in range(ITERS)]
    for k in range(ITERS):
        num = jnp.zeros((8, 128), F32)
        den = jnp.zeros((8, 128), F32)
        for i in range(k + 1):
            for j in range(k + 1):
                both = left_over[i] * left_over[j]
                num = num + both * table[i, j + 1]
                den = den + both * table[i + 1, j + 1]
        step = num / (den + rest)
        for i in range(k + 1):
            gained[i] = gained[i] + step * left_over[i]
        new = left_over + [jnp.zeros((8, 128), F32)]
        for i in range(k + 1):
            new[i + 1] = new[i + 1] - step * left_over[i]
        left_over = new
    gained = [by_column(value) * sigma for value in gained]
    left_over = [by_column(value) for value in left_over[1:]]

    def outcome(leaf):
        solved = gained[0] * ks[0, leaf]
        residual = ks[0, leaf]
        for i in range(1, ITERS):
            solved = solved + gained[i] * ks[i, leaf]
        for i in range(1, ITERS + 1):
            residual = residual + left_over[i - 1] * ks[i, leaf]
        return solved.astype(BF16), residual.astype(BF16)

    for leaf in range(2):
        otheirs[0, leaf], otheirs[1, leaf] = outcome(2 * (1 - core) + leaf)
    swap = remote(otheirs, omine.at[core], xs_sem.at[6], xr_sem.at[6], mate)
    swap.start()
    for leaf in range(2):
        omine[core, 0, leaf], omine[core, 1, leaf] = outcome(2 * core + leaf)
    sums_sent(0)
    sums_sent(1)
    sums_sent(2)
    for earlier in swaps:
        earlier.wait_send()
    rest = hd1.at[pl.ds(1, 7)]
    remote(rest, rest, xs_sem.at[7], xr_sem.at[7], mate).wait_send()
    rest = hd2.at[core, pl.ds(1, 7)]
    remote(rest, rest, xs_sem.at[8], xr_sem.at[8], mate).wait_send()
    lift4.wait_send()
    lift_swap.wait_send()
    rest = d1x.at[pl.ds(1, 7)]
    remote(rest, rest, xs_sem.at[11], xr_sem.at[11], mate).wait_send()
    remote(hd2.at[core], hd2.at[core], xs_sem.at[10], xr_sem.at[10], mate).wait_send()
    for k in range(ITERS):
        remote(s1.at[k, pl.ds(1, 7)], s1.at[k, pl.ds(1, 7)], ss.at[0, k], rs.at[0, k], mate).wait_send()
        remote(d2.at[k, pl.ds(1, 31)], d2.at[k, pl.ds(1, 31)], ss.at[1, k], rs.at[1, k], mate).wait_send()
        remote(d3.at[k, pl.ds(1, 7)], d3.at[k, pl.ds(1, 7)], ss.at[2, k], rs.at[2, k], mate).wait_send()
        remote(db.at[k, pl.ds(1, 3)], db.at[k, pl.ds(1, 3)], ss.at[3, k], rs.at[3, k], mate).wait_send()
    swap.wait_recv()
    writes = []
    for which, out in ((0, out_a), (1, out_b)):
        for leaf in range(2):
            both = jnp.concatenate([omine[0, which, leaf], omine[1, which, leaf]], axis=0)
            outs_v[which, leaf * LEAF:(leaf + 1) * LEAF, :] = both.astype(F32).T.astype(BF16)
        write = pltpu.make_async_copy(outs_v.at[which], out, load_sem.at[which])
        write.start()
        writes.append(write)
    for write in writes:
        write.wait()
    swap.wait_send()


def per_device(rhs, diag_blocks, leaf_bases, leaf_up, chain_up, chain_pair, node_ranks):
    anywhere = pl.BlockSpec(memory_space=pl.ANY)
    vm = pltpu.VMEM
    dma = pltpu.SemaphoreType.DMA
    n = ITERS
    return pl.pallas_call(
        kernel,
        out_shape=(jax.ShapeDtypeStruct((2 * LEAF, 2 * HALF), BF16),) * 2,
        in_specs=[anywhere] * 6 + [pl.BlockSpec(memory_space=pltpu.SMEM)],
        out_specs=(anywhere, anywhere),
        scratch_shapes=[
            vm((2 * LEAF, 2 * HALF), BF16),
            vm((4, LEAF, LEAF), BF16),
            vm((2, LEAF, R), BF16),
            vm((2, R, R), BF16),
            vm((4, LEAF, R), BF16),
            vm((4, R, R), BF16),
            vm((2, R, R), BF16),
            vm((2, R, R), BF16),
            vm((8, R, R), BF16),
            vm((10, R, R), BF16),
            vm((2, 2, HALF, LEAF), BF16),
            vm((4, HALF, LEAF), BF16),
            vm((4, R, LEAF), BF16),
            vm((4, R, R), BF16),
            vm((2, R, R), BF16),
            vm((R, R), BF16),
            vm((4, LEAF, R), BF16),
            vm((4, R, LEAF), BF16),
            vm((4, LEAF, R), BF16),
            vm((4, R, LEAF), BF16),
            vm((R, R), BF16),
            vm((2 * R, R), BF16),
            vm((2 * R, 5 * R), BF16),
            vm((5 * R, 2 * R), BF16),
            vm((2, 2, 128, R), BF16),
            vm((2, R, R), BF16),
            vm((2, R, R), BF16),
            vm((R, R), BF16),
            vm((2 * R, R), BF16),
            vm((HALF, R), F32),
            vm((R, 4 * R), BF16),
            vm((8, 16, 128), BF16),
            vm((8, 16, 128), BF16),
            vm((n + 1, 4, HALF, LEAF), F32),
            vm((4, HALF, LEAF), BF16),
            vm((4, HALF, LEAF), F32),
            vm((HALF, 128), F32),
            vm((8, 128), F32),
            vm((4, 128), F32),
            vm((8, 4, 128), F32),
            vm((32, 4, 128), F32),
            vm((4, 128), F32),
            vm((n, 8, 16, 128), BF16),
            vm((n, 8, 16, 128), BF16),
            vm((n, 5, 16, 128), BF16),
            vm((n, 32, 16, 128), BF16),
            vm((n, 2, 16, 128), BF16),
            vm((n, 8, 16, 128), BF16),
            vm((n, 2, HALF, R), BF16),
            vm((n, 4, HALF, R), BF16),
            vm((2, 8, 128), F32),
            vm((2, 8, 8, 128), F32),
            vm((2, 32, 8, 128), F32),
            vm((2, 8, 128), F32),
            vm((2, 8, 16, R), BF16),
            vm((8, 16, R), BF16),
            vm((2, 8, 2, 16, R), BF16),
            vm((8, 2 * R), F32),
            vm((2, 2, 2, HALF, LEAF), BF16),
            vm((2, 2, HALF, LEAF), BF16),
            vm((2, 2 * LEAF, 2 * HALF), BF16),
            vm((8, 2 * R), F32),
            dma((7,)),
            dma((13,)),
            dma((13,)),
            dma((6, n)),
            dma((6, n)),
        ],
        compiler_params=pltpu.CompilerParams(
            collective_id=0, has_side_effects=True, vmem_limit_bytes=56 * 2**20
        ),
        name="sweeps",
    )(rhs, diag_blocks, leaf_bases, leaf_up, chain_up, chain_pair, node_ranks)


def solution(mesh):
    return jax.shard_map(
        per_device,
        mesh=mesh,
        in_specs=(
            P("leaf", None),
            P("leaf", None, None),
            P("leaf", None, None),
            P("leaf", None, None),
            P("leaf", None, None, None),
            P("leaf", None, None, None),
            P("leaf", None),
        ),
        out_specs=(P("leaf", None), P("leaf", None)),
        check_vma=False,
    )
```
